256 devices in a mesh: grp: 4 (over x), sub: 64 (over z, y, core).
Axes of the slice: x: 4, y: 4, z: 8, core: 2. Of those that a mesh axis runs over, the one named last changes fastest.
Arguments:
- spectra: float32 [256, 6, 512, 512], P(('grp', 'sub')), may hold values from -0.046875 to 0.046875
- legendre: bfloat16 [512, 128, 512], P('sub'), may hold values from -6 to 6
- degree_counts: int32 [4, 512], replicated, may hold values from 1 to 512, as said below
Outputs:
- forcing: bfloat16 [256, 3, 128, 3072], P(('grp', 'sub'))
The draws below stay inside these ranges and needn't reach their ends.
Inputs may be any that keep to these rules, and one draw needn't show every extreme that they name: degree_counts[g, i] never exceeds 512 - i; within a group it falls by one from one order to the next until it reaches 1.
All inputs are finite; a program needn't handle non-finite values.
Results may differ from the reference program's by a relative error of at most 0.0064.
Values may be sent and summed in bfloat16 or wider, within the bound.
A program may use at most 128 MiB of HBM per device.

```python
import math
import jax
import jax.numpy as jnp
from jax import lax

DEGREE_LIMIT = 1024
MW = 512
LOWEST_ORDER = 512
NLAT = 1536
NLAT_W = 128
LONGITUDE_COUNT = 3072
GROUPS = 4
SHELLS = 256


def draw_degree_counts(key, part):
    key = jax.random.fold_in(key, 11)
    key_limits, key_widest = jax.random.split(key)
    limits = jax.random.randint(key_limits, (GROUPS,), MW // 2, MW + 1)
    widest = jax.random.randint(key_widest, (), 0, GROUPS)
    limits = jnp.where(jnp.arange(GROUPS) == widest, MW, limits)
    return jnp.maximum(limits[:, None] - jnp.arange(MW)[None, :], 1).astype(jnp.int32)


def levels(key, shape, pieces, low, high):
    loudness, own = 1.0, jax.random.fold_in(key, 6)
    for axis_at, blocks in pieces:
        steps = jnp.exp(jax.random.uniform(jax.random.fold_in(own, axis_at), (blocks,), jnp.float32, low / len(pieces), high / len(pieces)))
        loudness = loudness * jnp.repeat(steps, shape[axis_at] // blocks).reshape([-1 if axis == axis_at else 1 for axis in range(len(shape))])
    return loudness


def centred(rng, dims, width, most, cuts=(), kind=jnp.bfloat16):
    loudness = levels(rng, dims, cuts, -0.22, 0.18) if cuts else 1.0
    entries = jax.random.normal(rng, dims, jnp.float32) * width * loudness
    return jnp.minimum(jnp.maximum(entries, -most), most).astype(kind)


def setup_inputs(seed: int = 0) -> dict:
    seeds = jax.random.split(jax.random.key(seed), 4)
    return {
        "spectra": centred(seeds[0], (SHELLS, 6, MW, MW), (1.5 / MW), 0.046875, ((0, 256),), jnp.float32),
        "legendre": centred(seeds[1], (MW, NLAT_W, MW), 1.0, 6.0, ((0, 64),)),
        "degree_counts": draw_degree_counts(jax.random.fold_in(seeds[3], 71), 0),
    }


RADIUS_IN = 0.35 / 0.65
ELSASSER = 0.5


def forcing_terms(velocity, differ, radius, cos_theta, sin_theta):
    flow_radial = velocity[..., 0, :, :]
    flow_polar = velocity[..., 1, :, :]
    flow_azimuth = velocity[..., 2, :, :]
    cross_radial = -sin_theta * flow_azimuth
    cross_polar = -cos_theta * flow_azimuth
    cross_azimuth = cos_theta * flow_polar + sin_theta * flow_radial
    strength = (RADIUS_IN / radius) ** 3
    field_radial = 2.0 * strength * cos_theta
    field_polar = strength * sin_theta
    aligned = flow_radial * field_radial + flow_polar * field_polar
    squared = field_radial * field_radial + field_polar * field_polar
    force_radial = -cross_radial + ELSASSER * (aligned * field_radial - squared * flow_radial) - flow_radial * differ[..., 0, :, :]
    force_polar = -cross_polar + ELSASSER * (aligned * field_polar - squared * flow_polar) - flow_radial * differ[..., 1, :, :]
    force_azimuth = -cross_azimuth - ELSASSER * squared * flow_azimuth - flow_radial * differ[..., 2, :, :]
    return jnp.stack([force_radial, force_polar, force_azimuth], axis=-3).astype(jnp.bfloat16)


def reference(spectra, legendre, degree_counts):
    shells_all = spectra.shape[0]
    per_group = shells_all // GROUPS
    degree_pos = jnp.arange(MW, dtype=jnp.int32)
    legendre_wide = legendre.astype(jnp.float32)

    def one_shell(shell_index):
        coeffs = lax.dynamic_index_in_dim(spectra, shell_index, 0, keepdims=False)
        counts = lax.dynamic_index_in_dim(degree_counts, shell_index // per_group, 0, keepdims=False)
        kept_mask = degree_pos[None, :] < counts[:, None]
        coeffs = jnp.where(kept_mask[None], coeffs, 0.0).astype(jnp.bfloat16)
        coeffs = lax.optimization_barrier(coeffs).astype(jnp.float32)
        fourier = jnp.einsum("cmj,mkj->cmk", coeffs, legendre_wide).astype(jnp.bfloat16)
        fourier = lax.optimization_barrier(fourier).astype(jnp.float32)
        fourier = fourier.reshape(3, 2, MW, NLAT_W)
        velocity_spectrum = (fourier[:, 0] + 1j * fourier[:, 1]) * (LONGITUDE_COUNT / 2)
        velocity_spectrum = jnp.swapaxes(velocity_spectrum, 1, 2)
        padded_spectrum = jnp.zeros((3, NLAT_W, LONGITUDE_COUNT // 2 + 1), dtype=velocity_spectrum.dtype)
        padded_spectrum = padded_spectrum.at[:, :, LOWEST_ORDER:DEGREE_LIMIT].set(velocity_spectrum)
        return jnp.fft.irfft(padded_spectrum, n=LONGITUDE_COUNT, axis=-1).astype(jnp.float32)

    velocity = lax.map(one_shell, jnp.arange(shells_all, dtype=jnp.int32))
    colatitude = math.pi * (jnp.arange(NLAT_W, dtype=jnp.float32) + ((NLAT - NLAT_W) // 2) + 0.5) / NLAT
    cos_theta = jnp.cos(colatitude)[:, None]
    sin_theta = jnp.sin(colatitude)[:, None]

    def shell_force(shell_index):
        current = velocity[shell_index]
        outer_shell = velocity[jnp.minimum(shell_index + 1, shells_all - 1)]
        inner_shell = velocity[jnp.maximum(shell_index - 1, 0)]
        differ = jnp.where(shell_index == 0, outer_shell - current,
                           jnp.where(shell_index == shells_all - 1, current - inner_shell,
                                     0.5 * (outer_shell - inner_shell)))
        radius = RADIUS_IN + (shell_index.astype(jnp.float32) + 0.5) / shells_all
        return forcing_terms(current, differ, radius, cos_theta, sin_theta)

    return lax.map(shell_force, jnp.arange(shells_all, dtype=jnp.int32))
```

```python
import math

import jax
import jax.numpy as jnp
import numpy as np
from jax import lax
from jax.experimental import pallas as pl
from jax.experimental.pallas import tpu as pltpu
from jax.sharding import PartitionSpec as P

MESH = pl.DeviceIdType.MESH
BF16 = jnp.bfloat16
F32 = jnp.float32

LOWEST_ORDER = 512
NLAT = 1536
NLAT_W = 128
LONGITUDE_COUNT = 3072
HALF = LONGITUDE_COUNT // 2
RADIUS_IN = 0.35 / 0.65
ELSASSER = 0.5
SHELLS = 256

GX, NZ, NQ = 4, 8, 8
PEERS = GX * NQ
PAIRS = NZ // 2
WIDTH = 640


def lanes_of(zb):
    return 512 - 128 * (zb // 2)


def order_permutation():
    p = np.zeros((192, 192), np.float32)
    for x in range(GX):
        for v in range(3):
            for o in range(2):
                for k in range(PAIRS):
                    for part in range(2):
                        p[x * 48 + v * 16 + o * 8 + k * 2 + part, k * 48 + (2 * v + part) * 8 + 2 * x + o] = 1
    return p


def fourier_table():
    x, q, h, k = np.meshgrid(np.arange(GX), np.arange(NQ), np.arange(2), np.arange(PAIRS), indexing="ij")
    zb = np.where(h == 0, k, NZ - 1 - k)
    first = (64 * zb + 8 * q + 2 * x).reshape(-1)
    n = np.arange(HALF)
    out = np.zeros((2, first.size, 2, HALF), np.float32)
    for o in range(2):
        phase = ((LOWEST_ORDER + first + o)[:, None] * n[None, :]) % LONGITUDE_COUNT
        angle = phase * (2.0 * math.pi / LONGITUDE_COUNT)
        out[o, :, 0] = np.cos(angle)
        out[o, :, 1] = -np.sin(angle)
    return out.reshape(2, 2 * first.size, HALF)


def exchange_kernel(
    counts, spectra, legendre, perm, out,
    rows, packed, sends, recv, basis, fd, low, high,
    rows_sem, own_sem, spec_send, spec_recv, leg_send, leg_recv,
    end_send, end_recv, out_send, out_recv, local_sem,
):
    gx = lax.axis_index("grp")
    sub = lax.axis_index("sub")
    z, q = sub // NQ, sub % NQ
    me = gx * NQ + q
    up, down = (z + 1) % NZ, (z + NZ - 1) % NZ

    def peer(x, qq):
        return (x, z * NQ + qq)

    def along(zz):
        return (gx, zz * NQ + q)

    def row_copies(qq):
        return [
            pltpu.make_async_copy(
                spectra.at[0, :, pl.ds(64 * zb + 8 * qq, 8), pl.ds(0, lanes_of(zb))],
                rows.at[:, pl.ds(64 * zb + 8 * qq, 8), pl.ds(0, lanes_of(zb))],
                rows_sem.at[qq, zb],
            )
            for zb in range(NZ)
        ]

    @pl.loop(0, NQ)
    def _(i):
        for copy in row_copies((q + i) % NQ):
            copy.start()

    own = pltpu.make_async_copy(legendre.at[pl.ds(2 * gx, 2)], basis.at[z], own_sem)
    own.start()

    barrier = pltpu.get_barrier_semaphore()

    @pl.loop(0, PEERS)
    def _(i):
        @pl.when(i != me)
        def _():
            pl.semaphore_signal(barrier, inc=1, device_id=peer(i // NQ, i % NQ), device_id_type=MESH)

    for zz in (up, down):
        pl.semaphore_signal(barrier, inc=1, device_id=along(zz), device_id_type=MESH)

    limit = counts[gx, 0]

    def pack(qq):
        for copy in row_copies(qq):
            copy.wait()
        for k in range(PAIRS):
            parts = []
            for zb in (k, NZ - 1 - k):
                width = lanes_of(zb)
                block = rows[:, pl.ds(64 * zb + 8 * qq, 8), pl.ds(0, width)]
                order = lax.broadcasted_iota(jnp.int32, (8, width), 0) + (64 * zb + 8 * qq)
                degree = lax.broadcasted_iota(jnp.int32, (8, width), 1)
                keep = degree < jnp.maximum(limit - order, 1)
                block = jnp.where(keep[None], block, 0.0)
                parts.append(block.reshape(48, width))
            packed[pl.ds(48 * k, 48), :] = jnp.concatenate(parts, axis=1).astype(BF16)
        mixed = jnp.dot(perm[...], packed[...], preferred_element_type=F32)
        sends[qq] = mixed.astype(BF16).reshape(GX, 48, WIDTH)

    def spec_copy(x, qq):
        to = x * NQ + qq
        return pltpu.make_async_remote_copy(
            src_ref=sends.at[qq, x],
            dst_ref=recv.at[me],
            send_sem=spec_send.at[to],
            recv_sem=spec_recv.at[me],
            device_id=peer(x, qq),
            device_id_type=MESH,
        )

    def spec_arrival(frm):
        return pltpu.make_async_remote_copy(
            src_ref=sends.at[0, 0],
            dst_ref=recv.at[frm],
            send_sem=spec_send.at[frm],
            recv_sem=spec_recv.at[frm],
            device_id=peer(frm // NQ, frm % NQ),
            device_id_type=MESH,
        )

    def send_spec(qq):
        @pl.loop(0, GX)
        def _(j):
            x = (gx + j) % GX

            @pl.when(x * NQ + qq != me)
            def _():
                spec_copy(x, qq).start()

    def leg_copies(step, way):
        zb = (z + NZ - step) % NZ if way == 0 else (z + step) % NZ
        target = up if way == 0 else down
        orders = pl.ds(0, 2) if step < 3 else pl.ds(way, 1)
        result = []
        for t in range(4):
            lanes = pl.ds(128 * t, 128)
            if step == 0:
                src = legendre.at[pl.ds(2 * gx, 2), :, lanes]
            else:
                src = basis.at[zb, orders, :, lanes]
            copy = pltpu.make_async_remote_copy(
                src_ref=src,
                dst_ref=basis.at[zb, orders, :, lanes],
                send_sem=leg_send.at[way, step, t],
                recv_sem=leg_recv.at[way, step, t],
                device_id=along(target),
                device_id_type=MESH,
            )
            result.append((t < 4 - zb // 2, copy))
        return result

    def leg_arrivals(step, way):
        zb = (z + NZ - step - 1) % NZ if way == 0 else (z + step + 1) % NZ
        orders = pl.ds(0, 2) if step < 3 else pl.ds(way, 1)
        result = []
        for t in range(4):
            lanes = pl.ds(128 * t, 128)
            copy = pltpu.make_async_remote_copy(
                src_ref=basis.at[zb, orders, :, lanes],
                dst_ref=basis.at[zb, orders, :, lanes],
                send_sem=leg_send.at[way, step, t],
                recv_sem=leg_recv.at[way, step, t],
                device_id=along(down if way == 0 else up),
                device_id_type=MESH,
            )
            result.append((t < 4 - zb // 2, copy))
        return result

    def leg_start(step):
        for way in range(2):
            for here, copy in leg_copies(step, way):
                @pl.when(here)
                def _():
                    copy.start()

    def leg_wait(step):
        for way in range(2):
            for here, copy in leg_arrivals(step, way):
                @pl.when(here)
                def _():
                    copy.wait_recv()

    pack(q)
    pl.semaphore_wait(barrier, PEERS - 1 + 2)
    leg_start(0)
    send_spec(q)
    mine = pltpu.make_async_copy(sends.at[q, gx], recv.at[me], local_sem.at[0])
    mine.start()

    @pl.loop(1, 4)
    def _(i):
        pack((q + i) % NQ)
        send_spec((q + i) % NQ)

    leg_wait(0)
    leg_start(1)

    @pl.loop(4, NQ)
    def _(i):
        pack((q + i) % NQ)
        send_spec((q + i) % NQ)

    leg_wait(1)
    leg_start(2)
    leg_wait(2)
    leg_start(3)
    own.wait()
    mine.wait()
    leg_wait(3)

    def out_copy(x, qq, what):
        to = x * NQ + qq
        return pltpu.make_async_remote_copy(
            src_ref=fd.at[x, qq, what],
            dst_ref=out.at[what, :, :, me],
            send_sem=out_send.at[to],
            recv_sem=out_recv.at[me],
            device_id=peer(x, qq),
            device_id_type=MESH,
        )

    def end_copies(x):
        return [
            pltpu.make_async_remote_copy(
                src_ref=fd.at[x, NQ - 1, 0],
                dst_ref=low.at[x],
                send_sem=end_send.at[0, x],
                recv_sem=end_recv.at[0, x],
                device_id=along(up),
                device_id_type=MESH,
            ),
            pltpu.make_async_remote_copy(
                src_ref=fd.at[x, 0, 0],
                dst_ref=high.at[x],
                send_sem=end_send.at[1, x],
                recv_sem=end_recv.at[1, x],
                device_id=along(down),
                device_id_type=MESH,
            ),
        ]

    rows384 = lax.broadcasted_iota(jnp.int32, (384, 128), 0)
    odd = rows384 % 16 >= 8
    pair_of = rows384 % 8 // 2

    @pl.loop(0, GX)
    def _(j):
        x = (gx + j) % GX

        @pl.loop(0, NQ)
        def _(i):
            @pl.when(x * NQ + i != me)
            def _():
                spec_arrival(x * NQ + i).wait_recv()

        total = [jnp.zeros((384, 128), F32)] * 2
        for k in range(PAIRS):
            first = lanes_of(k)
            for h, zb in enumerate((k, NZ - 1 - k)):
                width = lanes_of(zb)
                left = recv[pl.ds(x * NQ, NQ), :, pl.ds(h * first, width)].reshape(384, width)
                right = basis[zb, :, :, pl.ds(0, width)].reshape(256, width)
                both = lax.dot_general(left, right, (((1,), (1,)), ((), ())), preferred_element_type=F32)
                one = jnp.where(odd, both[:, 128:], both[:, :128])
                total[h] = jnp.where(pair_of == k, one, total[h])
        fourier = jnp.concatenate([t.reshape(NQ, 3, 2, 8, 128) for t in total], axis=3).astype(BF16)
        fd[x, :, 0] = fourier
        for copy in end_copies(x):
            copy.start()
        wide = fourier.astype(F32)
        fd[x, 1 : NQ - 1, 1] = (0.5 * (wide[2:] - wide[:-2])).astype(BF16)

        @pl.loop(0, NQ)
        def _(i):
            qq = (q + i) % NQ
            inner = (qq > 0) & (qq < NQ - 1)

            @pl.when((x * NQ + qq != me) & inner)
            def _():
                out_copy(x, qq, pl.ds(0, 2)).start()

            @pl.when((x * NQ + qq != me) & jnp.logical_not(inner))
            def _():
                out_copy(x, qq, pl.ds(0, 1)).start()

    for x in range(GX):
        for copy in end_copies(x):
            copy.wait_recv()

    for x in range(GX):
        bottom = fd[x, 0, 0].astype(F32)
        second = fd[x, 1, 0].astype(F32)
        below = low[x].astype(F32)
        before = low[x - 1].astype(F32) if x > 0 else 2.0 * bottom - second
        below = jnp.where(z == 0, before, below)
        fd[x, 0, 1] = (0.5 * (second - below)).astype(BF16)
        top = fd[x, NQ - 1, 0].astype(F32)
        last = fd[x, NQ - 2, 0].astype(F32)
        above = high[x].astype(F32)
        after = high[x + 1].astype(F32) if x < GX - 1 else 2.0 * top - last
        above = jnp.where(z == NZ - 1, after, above)
        fd[x, NQ - 1, 1] = (0.5 * (above - last)).astype(BF16)
        for qq in (0, NQ - 1):
            @pl.when(x * NQ + qq != me)
            def _():
                out_copy(x, qq, pl.ds(1, 1)).start()

    keep = pltpu.make_async_copy(fd.at[gx, q], out.at[:, :, :, me], local_sem.at[1])
    keep.start()
    keep.wait()

    @pl.loop(0, PEERS)
    def _(i):
        @pl.when(i != me)
        def _():
            out_arrival = pltpu.make_async_remote_copy(
                src_ref=fd.at[i // NQ, i % NQ],
                dst_ref=out.at[:, :, :, i],
                send_sem=out_send.at[i],
                recv_sem=out_recv.at[i],
                device_id=peer(i // NQ, i % NQ),
                device_id_type=MESH,
            )
            out_arrival.wait_recv()
            out_arrival.wait_send()
            spec_copy(i // NQ, i % NQ).wait_send()

    for x in range(GX):
        for copy in end_copies(x):
            copy.wait_send()
    for step in range(4):
        for way in range(2):
            for here, copy in leg_copies(step, way):
                @pl.when(here)
                def _():
                    copy.wait_send()


def exchange(counts, spectra, legendre, perm):
    return pl.pallas_call(
        exchange_kernel,
        out_shape=jax.ShapeDtypeStruct((2, 3, 2, PEERS, 16, 128), BF16),
        in_specs=[
            pl.BlockSpec(memory_space=pltpu.SMEM),
            pl.BlockSpec(memory_space=pl.ANY),
            pl.BlockSpec(memory_space=pl.ANY),
            pl.BlockSpec(memory_space=pltpu.VMEM),
        ],
        out_specs=pl.BlockSpec(memory_space=pl.ANY),
        scratch_shapes=[
            pltpu.VMEM((6, 512, 512), F32),
            pltpu.VMEM((192, WIDTH), BF16),
            pltpu.VMEM((NQ, GX, 48, WIDTH), BF16),
            pltpu.VMEM((PEERS, 48, WIDTH), BF16),
            pltpu.VMEM((NZ, 2, 128, 512), BF16),
            pltpu.VMEM((GX, NQ, 2, 3, 2, 16, 128), BF16),
            pltpu.VMEM((GX, 3, 2, 16, 128), BF16),
            pltpu.VMEM((GX, 3, 2, 16, 128), BF16),
            pltpu.SemaphoreType.DMA((NQ, NZ)),
            pltpu.SemaphoreType.DMA,
            pltpu.SemaphoreType.DMA((PEERS,)),
            pltpu.SemaphoreType.DMA((PEERS,)),
            pltpu.SemaphoreType.DMA((2, 4, 4)),
            pltpu.SemaphoreType.DMA((2, 4, 4)),
            pltpu.SemaphoreType.DMA((2, GX)),
            pltpu.SemaphoreType.DMA((2, GX)),
            pltpu.SemaphoreType.DMA((PEERS,)),
            pltpu.SemaphoreType.DMA((PEERS,)),
            pltpu.SemaphoreType.DMA((2,)),
        ],
        compiler_params=pltpu.CompilerParams(
            collective_id=0, has_side_effects=True, vmem_limit_bytes=40 * 2**20
        ),
        cost_estimate=pl.CostEstimate(flops=2 * 10**9, bytes_accessed=10**7, transcendentals=0),
    )(counts, spectra, legendre, perm)


TILE = 256
STEPS = HALF // TILE


def synthesis_kernel(field, geometry, fd, table, out, left, later):
    half = pl.program_id(1)

    @pl.when((pl.program_id(0) == 0) & (half == 0))
    def _():
        for o in range(2):
            for what in range(2):
                for v in range(3):
                    block = fd[what, v, o].reshape(512, 128)
                    left[o, pl.ds(128 * (3 * what + v), 128), :] = block.T

    squared = field[0]
    cos_theta = geometry[:, 0:1]
    sin_theta = geometry[:, 1:2]

    def terms(flow):
        radial, polar, azimuth = flow[0:128], flow[128:256], flow[256:384]
        slope = [flow[384:512], flow[512:640], flow[640:768]]
        mix = squared * cos_theta * sin_theta
        out[0, 0] = (
            sin_theta * azimuth + mix * polar - radial * (0.5 * squared * sin_theta * sin_theta + slope[0])
        ).astype(BF16)
        out[0, 1] = (
            cos_theta * azimuth + mix * radial - 2.0 * squared * cos_theta * cos_theta * polar - radial * slope[1]
        ).astype(BF16)
        total = 0.5 * squared * (4.0 * cos_theta * cos_theta + sin_theta * sin_theta)
        out[0, 2] = (-cos_theta * polar - total * azimuth - radial * (sin_theta + slope[2])).astype(BF16)

    @pl.when(half == 0)
    def _():
        even = jnp.dot(left[0], table[0], preferred_element_type=F32)
        odd = jnp.dot(left[1], table[1], preferred_element_type=F32)
        later[...] = even - odd
        terms(even + odd)

    @pl.when(half == 1)
    def _():
        terms(later[...])


def synthesis(field, geometry, fd, table):
    return pl.pallas_call(
        synthesis_kernel,
        grid=(STEPS, 2),
        out_shape=jax.ShapeDtypeStruct((1, 3, NLAT_W, LONGITUDE_COUNT), BF16),
        in_specs=[
            pl.BlockSpec(memory_space=pltpu.SMEM),
            pl.BlockSpec((NLAT_W, 2), lambda i, h: (0, 0)),
            pl.BlockSpec((2, 3, 2, PEERS, 16, 128), lambda i, h: (0, 0, 0, 0, 0, 0)),
            pl.BlockSpec((2, 512, TILE), lambda i, h: (0, 0, i)),
        ],
        out_specs=pl.BlockSpec((1, 3, NLAT_W, TILE), lambda i, h: (0, 0, 0, h * STEPS + i)),
        scratch_shapes=[
            pltpu.VMEM((2, 768, 512), BF16),
            pltpu.VMEM((768, TILE), F32),
        ],
        compiler_params=pltpu.CompilerParams(vmem_limit_bytes=40 * 2**20),
        cost_estimate=pl.CostEstimate(flops=3 * 10**9, bytes_accessed=7 * 10**6, transcendentals=0),
    )(field, geometry, fd, table)


def shards(spectra, legendre, degree_counts):
    perm = jnp.asarray(order_permutation(), BF16)
    table = jnp.asarray(fourier_table(), BF16)
    theta = np.pi * (np.arange(NLAT_W) + (NLAT - NLAT_W) // 2 + 0.5) / NLAT
    geometry = jnp.asarray(np.stack([np.cos(theta), np.sin(theta)], axis=1), F32)
    shell = lax.axis_index(("grp", "sub")).astype(F32)
    radius = RADIUS_IN + (shell + 0.5) / SHELLS
    field = ((RADIUS_IN / radius) ** 6).reshape(1)
    fd = exchange(degree_counts, spectra, legendre, perm)
    return synthesis(field, geometry, fd, table)


def solution(mesh):
    in_specs = (P(("grp", "sub"), None, None, None), P("sub", None, None), P())
    out_specs = P(("grp", "sub"), None, None, None)
    return jax.shard_map(shards, mesh=mesh, in_specs=in_specs, out_specs=out_specs, check_vma=False)
```

```python
import math

import jax
import jax.numpy as jnp
import numpy as np
from jax import lax
from jax.experimental import pallas as pl
from jax.experimental.pallas import tpu as pltpu
from jax.sharding import PartitionSpec as P

MESH = pl.DeviceIdType.MESH
BF16 = jnp.bfloat16
F32 = jnp.float32

LOWEST_ORDER = 512
NLAT = 1536
NLAT_W = 128
LONGITUDE_COUNT = 3072
HALF = LONGITUDE_COUNT // 2
RADIUS_IN = 0.35 / 0.65
ELSASSER = 0.5
SHELLS = 256

GX, NZ, NQ = 4, 8, 8
PEERS = GX * NQ
PAIRS = NZ // 2
WIDTH = 640


def lanes_of(zb):
    return 512 - 128 * (zb // 2)


def order_permutation():
    p = np.zeros((192, 192), np.float32)
    for x in range(GX):
        for v in range(3):
            for o in range(2):
                for k in range(PAIRS):
                    for part in range(2):
                        p[x * 48 + v * 16 + o * 8 + k * 2 + part, k * 48 + (2 * v + part) * 8 + 2 * x + o] = 1
    return p


def fourier_table():
    x, q, h, k = np.meshgrid(np.arange(GX), np.arange(NQ), np.arange(2), np.arange(PAIRS), indexing="ij")
    zb = np.where(h == 0, k, NZ - 1 - k)
    first = (64 * zb + 8 * q + 2 * x).reshape(-1)
    n = np.arange(HALF)
    out = np.zeros((2, first.size, 2, HALF), np.float32)
    for o in range(2):
        phase = ((LOWEST_ORDER + first + o)[:, None] * n[None, :]) % LONGITUDE_COUNT
        angle = phase * (2.0 * math.pi / LONGITUDE_COUNT)
        out[o, :, 0] = np.cos(angle)
        out[o, :, 1] = -np.sin(angle)
    return out.reshape(2, 2 * first.size, HALF)


def exchange_kernel(
    counts, spectra, legendre, perm, left,
    limits, mixer, rows, packed, sends, recv, basis, fd, low, high, field,
    limit_sem, mixer_sem, rows_sem, own_sem, spec_send, spec_recv, leg_send, leg_recv,
    end_send, end_recv, out_send, out_recv, local_sem,
):
    gx = lax.axis_index("grp")
    sub = lax.axis_index("sub")
    z, q = sub // NQ, sub % NQ
    me = gx * NQ + q
    up, down = (z + 1) % NZ, (z + NZ - 1) % NZ

    def peer(x, qq):
        return (x, z * NQ + qq)

    def along(zz):
        return (gx, zz * NQ + q)

    barrier = pltpu.get_barrier_semaphore()

    @pl.loop(0, PEERS)
    def _(i):
        @pl.when(i != me)
        def _():
            pl.semaphore_signal(barrier, inc=1, device_id=peer(i // NQ, i % NQ), device_id_type=MESH)

    for zz in (up, down):
        pl.semaphore_signal(barrier, inc=1, device_id=along(zz), device_id_type=MESH)

    limit_copy = pltpu.make_async_copy(counts, limits, limit_sem)
    limit_copy.start()
    mixer_copy = pltpu.make_async_copy(perm, mixer, mixer_sem)
    mixer_copy.start()

    def row_copies(qq):
        return [
            pltpu.make_async_copy(
                spectra.at[0, :, pl.ds(64 * zb + 8 * qq, 8), pl.ds(0, lanes_of(zb))],
                rows.at[:, pl.ds(64 * zb + 8 * qq, 8), pl.ds(0, lanes_of(zb))],
                rows_sem.at[qq, zb],
            )
            for zb in range(NZ)
        ]

    @pl.loop(0, NQ)
    def _(i):
        for copy in row_copies((q + i) % NQ):
            copy.start()

    own = pltpu.make_async_copy(legendre.at[pl.ds(2 * gx, 2)], basis.at[z], own_sem)
    own.start()

    def pack(qq):
        for copy in row_copies(qq):
            copy.wait()
        limit = limits[gx, 0]
        for k in range(PAIRS):
            parts = []
            for zb in (k, NZ - 1 - k):
                width = lanes_of(zb)
                block = rows[:, pl.ds(64 * zb + 8 * qq, 8), pl.ds(0, width)]
                order = lax.broadcasted_iota(jnp.int32, (8, width), 0) + (64 * zb + 8 * qq)
                degree = lax.broadcasted_iota(jnp.int32, (8, width), 1)
                keep = degree < jnp.maximum(limit - order, 1)
                block = jnp.where(keep[None], block, 0.0)
                parts.append(block.reshape(48, width))
            packed[pl.ds(48 * k, 48), :] = jnp.concatenate(parts, axis=1).astype(BF16)
        mixed = jnp.dot(mixer[...], packed[...], preferred_element_type=F32)
        sends[qq] = mixed.astype(BF16).reshape(GX, 48, WIDTH)

    def spec_copy(x, qq):
        return pltpu.make_async_remote_copy(
            src_ref=sends.at[qq, x],
            dst_ref=recv.at[q, gx],
            send_sem=spec_send.at[qq, x],
            recv_sem=spec_recv.at[q, gx],
            device_id=peer(x, qq),
            device_id_type=MESH,
        )

    def spec_arrival(x, qq):
        return pltpu.make_async_remote_copy(
            src_ref=sends.at[qq, x],
            dst_ref=recv.at[qq, x],
            send_sem=spec_send.at[qq, x],
            recv_sem=spec_recv.at[qq, x],
            device_id=peer(x, qq),
            device_id_type=MESH,
        )

    def send_spec(qq):
        @pl.loop(0, GX)
        def _(j):
            x = (gx + j) % GX

            @pl.when(x * NQ + qq != me)
            def _():
                spec_copy(x, qq).start()

    def leg_piece(step, way, t, arriving):
        shift = step + 1 if arriving else step
        zb = (z + NZ - shift) % NZ if way == 0 else (z + shift) % NZ
        onward = (up, down)[way]
        backward = (down, up)[way]
        orders = pl.ds(0, 2) if step < 3 else pl.ds(way, 1)
        lanes = pl.ds(128 * t, 128)
        src = basis.at[zb, orders, :, lanes]
        if step == 0 and not arriving:
            src = legendre.at[pl.ds(2 * gx, 2), :, lanes]
        copy = pltpu.make_async_remote_copy(
            src_ref=src,
            dst_ref=basis.at[zb, orders, :, lanes],
            send_sem=leg_send.at[way, step, t],
            recv_sem=leg_recv.at[way, step, t],
            device_id=along(backward if arriving else onward),
            device_id_type=MESH,
        )
        return t < 4 - zb // 2, copy

    def leg_first():
        for t in range(4):
            for way in range(2):
                here, copy = leg_piece(0, way, t, False)
                pl.when(here)(copy.start)

    def leg_forward(step):
        for t in range(4):
            for way in range(2):
                here, arrival = leg_piece(step, way, t, True)

                @pl.when(here)
                def _():
                    arrival.wait_recv()
                    if step < 3:
                        leg_piece(step + 1, way, t, False)[1].start()

    limit_copy.wait()
    mixer_copy.wait()
    pack(q)
    pl.semaphore_wait(barrier, PEERS - 1 + 2)
    leg_first()
    send_spec(q)
    mine = pltpu.make_async_copy(sends.at[q, gx], recv.at[q, gx], local_sem.at[0])
    mine.start()

    def pack_and_send(i):
        pack((q + i) % NQ)
        send_spec((q + i) % NQ)

    pl.loop(1, 4)(pack_and_send)
    leg_forward(0)
    pl.loop(4, 6)(pack_and_send)
    leg_forward(1)
    pl.loop(6, 8)(pack_and_send)
    leg_forward(2)
    leg_forward(3)
    own.wait()
    mine.wait()

    def out_copy(x, qq, what):
        return pltpu.make_async_remote_copy(
            src_ref=fd.at[qq, x, what],
            dst_ref=field.at[what, :, :, me],
            send_sem=out_send.at[what, qq, x],
            recv_sem=out_recv.at[what, q, gx],
            device_id=peer(x, qq),
            device_id_type=MESH,
        )

    def out_arrival(x, qq, what):
        return pltpu.make_async_remote_copy(
            src_ref=fd.at[qq, x, what],
            dst_ref=field.at[what, :, :, x * NQ + qq],
            send_sem=out_send.at[what, qq, x],
            recv_sem=out_recv.at[what, qq, x],
            device_id=peer(x, qq),
            device_id_type=MESH,
        )

    def send_out(qq, what):
        @pl.loop(0, GX)
        def _(j):
            x = (gx + j) % GX

            @pl.when(x * NQ + qq != me)
            def _():
                out_copy(x, qq, what).start()

    def low_copy():
        return pltpu.make_async_remote_copy(
            src_ref=fd.at[NQ - 1, :, 0],
            dst_ref=low,
            send_sem=end_send.at[0],
            recv_sem=end_recv.at[0],
            device_id=along(up),
            device_id_type=MESH,
        )

    def high_copy():
        return pltpu.make_async_remote_copy(
            src_ref=fd.at[0, :, 0],
            dst_ref=high,
            send_sem=end_send.at[1],
            recv_sem=end_recv.at[1],
            device_id=along(down),
            device_id_type=MESH,
        )

    rows192 = lax.broadcasted_iota(jnp.int32, (192, 128), 0)
    odd = rows192 % 16 >= 8
    pair_of = rows192 % 8 // 2

    def inner_difference(m):
        @pl.when((m > 0) & (m < NQ - 1))
        def _():
            outer = fd[m + 1, :, 0].astype(F32)
            inner = fd[m - 1, :, 0].astype(F32)
            fd[m, :, 1] = (0.5 * (outer - inner)).astype(BF16)
            send_out(m, 1)

    @pl.loop(0, NQ)
    def _(i):
        qq = (q + NQ - i) % NQ

        @pl.loop(0, GX)
        def _(x):
            @pl.when(x * NQ + qq != me)
            def _():
                spec_arrival(x, qq).wait_recv()

        total = [jnp.zeros((192, 128), F32)] * 2
        for k in range(PAIRS):
            first = lanes_of(k)
            for h, zb in enumerate((k, NZ - 1 - k)):
                width = lanes_of(zb)
                block = recv[qq, :, :, pl.ds(h * first, width)].reshape(192, width)
                right = basis[zb, :, :, pl.ds(0, width)].reshape(256, width)
                both = lax.dot_general(block, right, (((1,), (1,)), ((), ())), preferred_element_type=F32)
                one = jnp.where(odd, both[:, 128:], both[:, :128])
                total[h] = jnp.where(pair_of == k, one, total[h])
        fourier = jnp.concatenate([t.reshape(GX, 3, 2, 8, 128) for t in total], axis=3).astype(BF16)
        fd[qq, :, 0] = fourier
        send_out(qq, 0)

        @pl.when(qq == NQ - 1)
        def _():
            low_copy().start()

        @pl.when(qq == 0)
        def _():
            high_copy().start()

        @pl.when(i >= 2)
        def _():
            inner_difference((qq + 1) % NQ)

    inner_difference((q + 1) % NQ)
    inner_difference(q)
    low_copy().wait_recv()
    high_copy().wait_recv()

    for x in range(GX):
        bottom = fd[0, x, 0].astype(F32)
        second = fd[1, x, 0].astype(F32)
        before = low[x - 1].astype(F32) if x > 0 else 2.0 * bottom - second
        below = jnp.where(z == 0, before, low[x].astype(F32))
        fd[0, x, 1] = (0.5 * (second - below)).astype(BF16)
        top = fd[NQ - 1, x, 0].astype(F32)
        last = fd[NQ - 2, x, 0].astype(F32)
        after = high[x + 1].astype(F32) if x < GX - 1 else 2.0 * top - last
        above = jnp.where(z == NZ - 1, after, high[x].astype(F32))
        fd[NQ - 1, x, 1] = (0.5 * (above - last)).astype(BF16)
    send_out(0, 1)
    send_out(NQ - 1, 1)

    keep = pltpu.make_async_copy(fd.at[q, gx], field.at[:, :, :, me], local_sem.at[1])
    keep.start()
    keep.wait()

    for what in range(2):
        @pl.loop(0, PEERS)
        def _(i):
            @pl.when(i != me)
            def _():
                out_arrival(i // NQ, i % NQ, what).wait_recv()

        for o in range(2):
            for v in range(3):
                block = field[what, v, o].reshape(512, 128)
                left[o, pl.ds(128 * (3 * what + v), 128), :] = block.T

    @pl.loop(0, PEERS)
    def _(i):
        @pl.when(i != me)
        def _():
            x, qq = i // NQ, i % NQ
            out_copy(x, qq, 0).wait_send()
            out_copy(x, qq, 1).wait_send()
            spec_copy(x, qq).wait_send()

    low_copy().wait_send()
    high_copy().wait_send()
    for step in range(4):
        for t in range(4):
            for way in range(2):
                here, copy = leg_piece(step, way, t, False)
                pl.when(here)(copy.wait_send)


def exchange(counts, spectra, legendre, perm):
    return pl.pallas_call(
        exchange_kernel,
        out_shape=jax.ShapeDtypeStruct((2, 768, 512), BF16),
        in_specs=[pl.BlockSpec(memory_space=pl.ANY)] * 4,
        out_specs=pl.BlockSpec(memory_space=pltpu.VMEM),
        scratch_shapes=[
            pltpu.SMEM((GX, 512), jnp.int32),
            pltpu.VMEM((192, 192), BF16),
            pltpu.VMEM((6, 512, 512), F32),
            pltpu.VMEM((192, WIDTH), BF16),
            pltpu.VMEM((NQ, GX, 48, WIDTH), BF16),
            pltpu.VMEM((NQ, GX, 48, WIDTH), BF16),
            pltpu.VMEM((NZ, 2, 128, 512), BF16),
            pltpu.VMEM((NQ, GX, 2, 3, 2, 16, 128), BF16),
            pltpu.VMEM((GX, 3, 2, 16, 128), BF16),
            pltpu.VMEM((GX, 3, 2, 16, 128), BF16),
            pltpu.VMEM((2, 3, 2, PEERS, 16, 128), BF16),
            pltpu.SemaphoreType.DMA,
            pltpu.SemaphoreType.DMA,
            pltpu.SemaphoreType.DMA((NQ, NZ)),
            pltpu.SemaphoreType.DMA,
            pltpu.SemaphoreType.DMA((NQ, GX)),
            pltpu.SemaphoreType.DMA((NQ, GX)),
            pltpu.SemaphoreType.DMA((2, 4, 4)),
            pltpu.SemaphoreType.DMA((2, 4, 4)),
            pltpu.SemaphoreType.DMA((2,)),
            pltpu.SemaphoreType.DMA((2,)),
            pltpu.SemaphoreType.DMA((2, NQ, GX)),
            pltpu.SemaphoreType.DMA((2, NQ, GX)),
            pltpu.SemaphoreType.DMA((2,)),
        ],
        compiler_params=pltpu.CompilerParams(
            collective_id=0, has_side_effects=True, vmem_limit_bytes=57 * 2**20
        ),
        cost_estimate=pl.CostEstimate(flops=2 * 10**9, bytes_accessed=10**7, transcendentals=0),
    )(counts, spectra, legendre, perm)


TILE = 256
STEPS = HALF // TILE
CHUNK = 16


def synthesis_kernel(field, geometry, left, table, out, factors, waves, stage, sems):
    squared = field[0]
    cos_theta = geometry[0]
    sin_theta = geometry[1]
    factors[0] = cos_theta
    factors[1] = sin_theta
    factors[2] = squared * cos_theta * sin_theta
    factors[3] = 0.5 * squared * sin_theta * sin_theta
    factors[4] = 2.0 * squared * cos_theta * cos_theta
    factors[5] = 0.5 * squared * (4.0 * cos_theta * cos_theta + sin_theta * sin_theta)

    def ship(i, h):
        return pltpu.make_async_copy(
            stage.at[i, h],
            out.at[0, :, :, pl.ds(h * HALF + i * TILE, TILE)],
            sems.at[i, h],
        )

    def wide(value):
        return jnp.concatenate([value] * (TILE // 128), axis=1)

    for i in range(STEPS):
        columns = pl.ds(i * TILE, TILE)
        for o in range(2):
            waves[i % 2, o] = jnp.dot(left[o], table[o, :, columns], preferred_element_type=F32)
        for r in range(0, NLAT_W, CHUNK):
            here = pl.ds(r, CHUNK)
            cos_w, sin_w, mix, own, twice, total = (wide(factors[n, here, :]) for n in range(6))
            even = [waves[i % 2, 0, pl.ds(128 * n + r, CHUNK), :] for n in range(6)]
            odd = [waves[i % 2, 1, pl.ds(128 * n + r, CHUNK), :] for n in range(6)]
            for h in range(2):
                flow = [a + b if h == 0 else a - b for a, b in zip(even, odd)]
                radial, polar, azimuth = flow[:3]
                stage[i, h, 0, here, :] = (
                    sin_w * azimuth + mix * polar - radial * (own + flow[3])
                ).astype(BF16)
                stage[i, h, 1, here, :] = (
                    cos_w * azimuth - twice * polar + radial * (mix - flow[4])
                ).astype(BF16)
                stage[i, h, 2, here, :] = (
                    -(cos_w * polar + total * azimuth + radial * (sin_w + flow[5]))
                ).astype(BF16)
        for h in range(2):
            ship(i, h).start()
    for i in range(STEPS):
        for h in range(2):
            ship(i, h).wait()


def synthesis(field, geometry, left, table):
    return pl.pallas_call(
        synthesis_kernel,
        out_shape=jax.ShapeDtypeStruct((1, 3, NLAT_W, LONGITUDE_COUNT), BF16),
        in_specs=[
            pl.BlockSpec(memory_space=pltpu.SMEM),
            pl.BlockSpec(memory_space=pltpu.VMEM),
            pl.BlockSpec(memory_space=pltpu.VMEM),
            pl.BlockSpec(memory_space=pltpu.VMEM),
        ],
        out_specs=pl.BlockSpec(memory_space=pl.ANY),
        scratch_shapes=[
            pltpu.VMEM((6, NLAT_W, 128), F32),
            pltpu.VMEM((2, 2, 768, TILE), F32),
            pltpu.VMEM((STEPS, 2, 3, NLAT_W, TILE), BF16),
            pltpu.SemaphoreType.DMA((STEPS, 2)),
        ],
        compiler_params=pltpu.CompilerParams(vmem_limit_bytes=32 * 2**20),
        cost_estimate=pl.CostEstimate(flops=3 * 10**9, bytes_accessed=7 * 10**6, transcendentals=0),
    )(field, geometry, left, table)


def shards(spectra, legendre, degree_counts):
    perm = jnp.asarray(order_permutation(), BF16)
    table = jnp.asarray(fourier_table(), BF16)
    theta = np.pi * (np.arange(NLAT_W) + (NLAT - NLAT_W) // 2 + 0.5) / NLAT
    geometry = np.repeat(np.stack([np.cos(theta), np.sin(theta)])[:, :, None], 128, axis=2)
    geometry = jnp.asarray(geometry, F32)
    shell = lax.axis_index(("grp", "sub")).astype(F32)
    radius = RADIUS_IN + (shell + 0.5) / SHELLS
    field = ((RADIUS_IN / radius) ** 6).reshape(1)
    left = exchange(degree_counts, spectra, legendre, perm)
    return synthesis(field, geometry, left, table)


def solution(mesh):
    in_specs = (P(("grp", "sub"), None, None, None), P("sub", None, None), P())
    out_specs = P(("grp", "sub"), None, None, None)
    return jax.shard_map(shards, mesh=mesh, in_specs=in_specs, out_specs=out_specs, check_vma=False)
```

```python
import math

import jax
import jax.numpy as jnp
import numpy as np
from jax import lax
from jax.experimental import pallas as pl
from jax.experimental.pallas import tpu as pltpu
from jax.sharding import PartitionSpec as P

MESH = pl.DeviceIdType.MESH
BF16 = jnp.bfloat16
F32 = jnp.float32

LOWEST_ORDER = 512
NLAT = 1536
NLAT_W = 128
LONGITUDE_COUNT = 3072
HALF = LONGITUDE_COUNT // 2
RADIUS_IN = 0.35 / 0.65
ELSASSER = 0.5
SHELLS = 256

GX, NZ, NQ = 4, 8, 8
PEERS = GX * NQ
PAIRS = NZ // 2
DEGREES = 512


def lanes_of(zb):
    return 512 - 128 * (zb // 2)


def order_permutation():
    p = np.zeros((192, 192), np.float32)
    for x in range(GX):
        for v in range(3):
            for o in range(2):
                for k in range(PAIRS):
                    for part in range(2):
                        p[x * 48 + v * 16 + o * 8 + k * 2 + part, k * 48 + (2 * v + part) * 8 + 2 * x + o] = 1
    return p


def fourier_table():
    x, q, h, k = np.meshgrid(np.arange(GX), np.arange(NQ), np.arange(2), np.arange(PAIRS), indexing="ij")
    block = 8 * k + q
    block = np.where(h == 0, block, np.where(block == 0, 32, 64 - block))
    first = (8 * block + 2 * x).reshape(-1)
    n = np.arange(HALF)
    out = np.zeros((2, first.size, 2, HALF), np.float32)
    for o in range(2):
        phase = ((LOWEST_ORDER + first + o)[:, None] * n[None, :]) % LONGITUDE_COUNT
        angle = phase * (2.0 * math.pi / LONGITUDE_COUNT)
        out[o, :, 0] = np.cos(angle)
        out[o, :, 1] = -np.sin(angle)
    return out.reshape(2, 2 * first.size, HALF)


def exchange_kernel(
    counts, spectra, legendre, perm, left,
    limits, mixer, rows, packed, sends, recv, sends_x, recv_x, basis, weights, weights_x, fd, low, high, field, turned,
    limit_sem, mixer_sem, rows_sem, own_send, own_recv, spec_send, spec_recv, x_send, x_recv, leg_send, leg_recv,
    end_send, end_recv, out_send, out_recv, left_sem,
):
    gx = lax.axis_index("grp")
    sub = lax.axis_index("sub")
    z, q = sub // NQ, sub % NQ
    me = gx * NQ + q
    y = q // 2
    up, down = (z + 1) % NZ, (z + NZ - 1) % NZ
    mirror = (NQ - q) % NQ
    column = jnp.where(z < PAIRS, q, mirror)

    def peer(x, qq):
        return (x, z * NQ + qq)

    def along(zz, qq):
        return (gx, zz * NQ + qq)

    barrier = pltpu.get_barrier_semaphore()

    @pl.loop(0, PEERS)
    def _(i):
        @pl.when(i != me)
        def _():
            pl.semaphore_signal(barrier, inc=1, device_id=peer(i // NQ, i % NQ), device_id_type=MESH)

    for zz in (up, down):
        for qq in (q, mirror):
            pl.semaphore_signal(barrier, inc=1, device_id=along(zz, qq), device_id_type=MESH)

    limit_copy = pltpu.make_async_copy(counts, limits, limit_sem)
    limit_copy.start()
    mixer_copy = pltpu.make_async_copy(perm, mixer, mixer_sem)
    mixer_copy.start()

    def pair_rows(k, qq):
        partner = 64 * (NZ - k) - 8 * qq
        if k == 0:
            partner = jnp.where(qq == 0, 256, partner)
        return pl.multiple_of(64 * k + 8 * qq, 8), pl.multiple_of(partner, 8)

    def row_copies(qq):
        copies = []
        for k in range(PAIRS):
            for h, (start, width) in enumerate(zip(pair_rows(k, qq), (lanes_of(k), 256))):
                copies.append(
                    pltpu.make_async_copy(
                        spectra.at[0, :, pl.ds(start, 8), pl.ds(0, width)],
                        rows.at[:, pl.ds(start, 8), pl.ds(0, width)],
                        rows_sem.at[qq, k, h],
                    )
                )
        return copies

    def place(i):
        return (y + i // 2) % (NQ // 2) * 2 + (q + i) % 2

    @pl.loop(0, NQ)
    def _(i):
        for copy in row_copies(place(i)):
            copy.start()

    def kept(start, width, valid):
        block = rows[:, pl.ds(start, 8), pl.ds(0, width)]
        order = lax.broadcasted_iota(jnp.int32, (8, width), 0) + start
        degree = lax.broadcasted_iota(jnp.int32, (8, width), 1)
        keep = degree < jnp.where(valid, jnp.maximum(limits[gx, 0] - order, 1), 0)
        return jnp.where(keep[None], block, 0.0).reshape(48, width)

    def pack(qq):
        for copy in row_copies(qq):
            copy.wait()
        for k in range(PAIRS):
            block = 8 * k + qq
            first, second = pair_rows(k, qq)
            width = lanes_of(k)
            one = kept(first, width, True)
            two = pltpu.roll(kept(second, 256, block > 0), (256 - 8 * block) % 256, 1)
            if width < DEGREES:
                one = jnp.concatenate([one, jnp.zeros((48, DEGREES - width), F32)], axis=1)
            both = jnp.concatenate([one[:, :256], one[:, 256:] + two], axis=1)
            packed[pl.ds(48 * k, 48), :] = both.astype(BF16)
        mixed = jnp.dot(mixer[...], packed[...], preferred_element_type=F32)
        sends[pl.ds(qq * GX, GX)] = mixed.astype(BF16).reshape(GX, 48, DEGREES)

        @pl.when(qq == 0)
        def _():
            alone = kept(256, 256, True).astype(BF16)
            zeros = jnp.zeros((96, 128), BF16)
            spread = jnp.concatenate([alone[:, :128], alone[:, 128:], zeros], axis=0)
            mixed = jnp.dot(mixer[...], spread, preferred_element_type=F32)
            sends_x[...] = mixed.astype(BF16).reshape(GX, 48, 128)

    def spec_copy(x, qq):
        return pltpu.make_async_remote_copy(
            src_ref=sends.at[qq * GX + x],
            dst_ref=recv.at[q, gx],
            send_sem=spec_send,
            recv_sem=spec_recv.at[y],
            device_id=peer(x, qq),
            device_id_type=MESH,
        )

    def spec_arrivals(yy):
        part = recv.at[pl.ds(2 * yy, 2)]
        return pltpu.make_async_copy(part, part, spec_recv.at[yy])

    def spec_departures():
        part = sends.at[pl.ds(0, PEERS - 1)]
        return pltpu.make_async_copy(part, part, spec_send)

    def x_copy(x):
        return pltpu.make_async_remote_copy(
            src_ref=sends_x.at[x],
            dst_ref=recv_x.at[q, gx],
            send_sem=x_send,
            recv_sem=x_recv.at[y],
            device_id=peer(x, 0),
            device_id_type=MESH,
        )

    def x_arrivals(yy):
        part = recv_x.at[pl.ds(2 * yy, 2)]
        return pltpu.make_async_copy(part, part, x_recv.at[yy])

    def x_departures(count):
        part = sends_x.at[pl.ds(0, count)]
        return pltpu.make_async_copy(part, part, x_send)

    def send_spec(qq):
        @pl.loop(0, GX)
        def _(j):
            x = (gx + j) % GX

            @pl.when(x * NQ + qq != me)
            def _():
                spec_copy(x, qq).start()

            @pl.when((x * NQ + qq != me) & (qq == 0))
            def _():
                x_copy(x).start()

    def pieces_of(zb):
        return 4 - zb // 2

    def mine_at(o, t):
        return legendre.at[2 * gx + o, :, pl.ds(128 * t, 128)]

    def leg_piece(o, step, way, t, arriving):
        shift = step + 1 if arriving else step
        zb = (z + NZ - shift) % NZ if way == 0 else (z + shift) % NZ
        onward, backward = (up, down) if way == 0 else (down, up)
        if arriving:
            target = along(backward, jnp.where(zb < PAIRS, q, mirror) if step == 0 else q)
        else:
            target = along(onward, column if step == 0 else q)
        copy = pltpu.make_async_remote_copy(
            src_ref=mine_at(o, t) if step == 0 and not arriving else basis.at[zb, o, t],
            dst_ref=basis.at[zb, o, t],
            send_sem=leg_send.at[o, way, step, t],
            recv_sem=leg_recv.at[o, way, step, t],
            device_id=target,
            device_id_type=MESH,
        )
        return t < pieces_of(zb), copy

    def goes(step, way, t):
        return step < 3 or way == t % 2

    def own_remote(o, t):
        return pltpu.make_async_remote_copy(
            src_ref=mine_at(o, t),
            dst_ref=basis.at[z, o, t],
            send_sem=own_send.at[o, t],
            recv_sem=own_recv.at[o, t],
            device_id=along(z, mirror),
            device_id_type=MESH,
        )

    def own_local(o, t):
        return pltpu.make_async_copy(mine_at(o, t), basis.at[z, o, t], own_recv.at[o, t])

    def own_each(o, remote, local):
        for t in range(4):
            here = t < pieces_of(z)

            @pl.when(here & (column != q))
            def _():
                remote(own_remote(o, t))

            if local is None:
                continue

            @pl.when(here & (column == q))
            def _():
                local(own_local(o, t))

    def leg_first(o):
        for t in range(4):
            for way in range(2):
                here, copy = leg_piece(o, 0, way, t, False)
                pl.when(here)(copy.start)
        own_each(o, lambda c: c.start(), lambda c: c.start())

    def leg_forward(o, step):
        for t in range(4):
            for way in range(2):
                if not goes(step, way, t):
                    continue
                here, arrival = leg_piece(o, step, way, t, True)

                @pl.when(here)
                def _():
                    arrival.wait_recv()
                    if step < 3 and goes(step + 1, way, t):
                        leg_piece(o, step + 1, way, t, False)[1].start()

    limit_copy.wait()
    mixer_copy.wait()
    pack(q)
    pl.semaphore_wait(barrier, PEERS - 1 + 4)
    leg_first(0)
    send_spec(q)
    pltpu.make_async_copy(sends.at[q * GX + gx], recv.at[q, gx], spec_recv.at[y]).start()

    @pl.when(q == 0)
    def _():
        pltpu.make_async_copy(sends_x.at[gx], recv_x.at[0, gx], x_recv.at[0]).start()

    @pl.when(q != 0)
    def _():
        recv_x[...] = jnp.zeros_like(recv_x)

    def pack_and_send(i):
        pack(place(i))
        send_spec(place(i))

    pl.loop(1, 4)(pack_and_send)
    leg_forward(0, 0)
    pl.loop(4, 6)(pack_and_send)
    leg_forward(0, 1)
    leg_first(1)
    pl.loop(6, 8)(pack_and_send)
    leg_forward(0, 2)
    leg_forward(1, 0)
    leg_forward(0, 3)
    leg_forward(1, 1)
    leg_forward(1, 2)
    own_each(0, lambda c: c.wait_recv(), lambda c: c.wait())

    def out_copy(x, qq, what, o):
        return pltpu.make_async_remote_copy(
            src_ref=fd.at[qq, x, what, o],
            dst_ref=field.at[what, o, :, me],
            send_sem=out_send.at[what, o],
            recv_sem=out_recv.at[what, o],
            device_id=peer(x, qq),
            device_id_type=MESH,
        )

    def out_arrivals(what, o):
        part = field.at[what, o]
        return pltpu.make_async_copy(part, part, out_recv.at[what, o])

    def out_departures(what, o):
        part = field.at[what, o, :, pl.ds(0, PEERS - 1)]
        return pltpu.make_async_copy(part, part, out_send.at[what, o])

    def send_out(qq, what, o):
        @pl.loop(0, GX)
        def _(j):
            x = (gx + j) % GX

            @pl.when(x * NQ + qq != me)
            def _():
                out_copy(x, qq, what, o).start()

        @pl.when(qq == q)
        def _():
            pltpu.make_async_copy(
                fd.at[q, gx, what, o], field.at[what, o, :, me], out_recv.at[what, o]
            ).start()

    def low_copy(o):
        return pltpu.make_async_remote_copy(
            src_ref=fd.at[NQ - 1, :, 0, o],
            dst_ref=low.at[o],
            send_sem=end_send.at[0, o],
            recv_sem=end_recv.at[0, o],
            device_id=along(up, q),
            device_id_type=MESH,
        )

    def high_copy(o):
        return pltpu.make_async_remote_copy(
            src_ref=fd.at[0, :, 0, o],
            dst_ref=high.at[o],
            send_sem=end_send.at[1, o],
            recv_sem=end_recv.at[1, o],
            device_id=along(down, q),
            device_id_type=MESH,
        )

    rows384 = lax.broadcasted_iota(jnp.int32, (384, 256), 0)
    pair_of = rows384 % 8 // 2

    def inner_differences(yy, o):
        @pl.when(yy < NQ // 2 - 1)
        def _():
            m = 2 * yy + 1
            outer = fd[pl.ds(m + 1, 2), :, 0, o].astype(F32)
            inner = fd[pl.ds(m - 1, 2), :, 0, o].astype(F32)
            fd[pl.ds(m, 2), :, 1, o] = (0.5 * (outer - inner)).astype(BF16)
            send_out(m, 1, o)
            send_out(m + 1, 1, o)

    def end_differences(o):
        low_copy(o).wait_recv()
        high_copy(o).wait_recv()
        for x in range(GX):
            bottom = fd[0, x, 0, o].astype(F32)
            second = fd[1, x, 0, o].astype(F32)
            before = low[o, x - 1].astype(F32) if x > 0 else 2.0 * bottom - second
            below = jnp.where(z == 0, before, low[o, x].astype(F32))
            fd[0, x, 1, o] = (0.5 * (second - below)).astype(BF16)
            top = fd[NQ - 1, x, 0, o].astype(F32)
            last = fd[NQ - 2, x, 0, o].astype(F32)
            after = high[o, x + 1].astype(F32) if x < GX - 1 else 2.0 * top - last
            above = jnp.where(z == NZ - 1, after, high[o, x].astype(F32))
            fd[NQ - 1, x, 1, o] = (0.5 * (above - last)).astype(BF16)
        send_out(0, 1, o)
        send_out(NQ - 1, 1, o)

    def build_weights(o):
        lane = lax.broadcasted_iota(jnp.int32, (128, DEGREES), 1)
        for k in range(PAIRS):
            block = 8 * k + q
            cut = DEGREES - 8 * block
            one = jnp.concatenate([basis[k, o, t] for t in range(4)], axis=1).astype(F32)
            weights[k, 0:128, :] = jnp.where(lane < cut, one, 0.0).astype(BF16)
            zb = jnp.where(q == 0, NZ - max(k, 1), NZ - 1 - k)
            two = jnp.concatenate([basis[zb, o, t] for t in range(2)], axis=1).astype(F32)
            two = pltpu.roll(two, (256 - 8 * block) % 256, 1)
            two = jnp.where(lane[:, 256:] >= cut, two, 0.0)
            weights[k, 128:256, :] = jnp.concatenate([jnp.zeros((128, 256), F32), two], axis=1).astype(BF16)
        weights_x[...] = jnp.concatenate([basis[PAIRS, o, t] for t in range(2)], axis=0)

    def coefficients(o):
        @pl.loop(0, NQ // 2)
        def _(i):
            yy = (y + NQ // 2 - i) % (NQ // 2)
            two = pl.ds(2 * yy, 2)
            if o == 0:
                spec_arrivals(yy).wait()

                @pl.when(q == 0)
                def _():
                    x_arrivals(yy).wait()

            block = recv[two].reshape(384, DEGREES)
            total = jnp.zeros((384, 256), F32)
            for k in range(PAIRS):
                both = lax.dot_general(block, weights[k], (((1,), (1,)), ((), ())), preferred_element_type=F32)
                total = jnp.where(pair_of == k, both, total)
            extra = lax.dot_general(
                recv_x[two].reshape(384, 128), weights_x[...], (((1,), (1,)), ((), ())), preferred_element_type=F32
            )
            extra = extra[:, :128] + pltpu.roll(extra[:, 128:], 382, 0)
            lower = total[:, :128]
            upper = total[:, 128:] + jnp.where(pair_of[:, :128] == 0, extra, 0.0)
            both = [part.reshape(2, GX, 3, 2, 8, 128)[:, :, :, o] for part in (lower, upper)]
            fd[two, :, 0, o] = jnp.concatenate(both, axis=3).astype(BF16)
            send_out(2 * yy, 0, o)
            send_out(2 * yy + 1, 0, o)

            @pl.when(yy == NQ // 2 - 1)
            def _():
                low_copy(o).start()

            @pl.when(yy == 0)
            def _():
                high_copy(o).start()

            @pl.when(i >= 1)
            def _():
                inner_differences(yy, o)

        inner_differences(y, o)

    build_weights(0)
    coefficients(0)
    leg_forward(1, 3)
    own_each(1, lambda c: c.wait_recv(), lambda c: c.wait())
    build_weights(1)
    end_differences(0)
    coefficients(1)
    end_differences(1)

    def left_copy(o):
        return pltpu.make_async_copy(turned.at[o], left.at[o], left_sem.at[o])

    spec_departures().wait()

    @pl.when(q == 0)
    def _():
        x_departures(GX - 1).wait()

    @pl.when(q != 0)
    def _():
        x_departures(GX).wait()

    for o in range(2):
        low_copy(o).wait_send()
        high_copy(o).wait_send()
        own_each(o, lambda c: c.wait_send(), None)
        for step in range(4):
            for t in range(4):
                for way in range(2):
                    if goes(step, way, t):
                        here, copy = leg_piece(o, step, way, t, False)
                        pl.when(here)(copy.wait_send)

    for o in range(2):
        for what in range(2):
            out_arrivals(what, o).wait()
            for v in range(3):
                block = field[what, o, v].reshape(512, 128)
                turned[o, pl.ds(128 * (3 * what + v), 128), :] = block.T
        left_copy(o).start()

    for o in range(2):
        for what in range(2):
            out_departures(what, o).wait()
        left_copy(o).wait()


def exchange(counts, spectra, legendre, perm):
    return pl.pallas_call(
        exchange_kernel,
        out_shape=jax.ShapeDtypeStruct((2, 768, 512), BF16),
        in_specs=[pl.BlockSpec(memory_space=pl.ANY)] * 4,
        out_specs=pl.BlockSpec(memory_space=pl.ANY),
        scratch_shapes=[
            pltpu.SMEM((GX, 512), jnp.int32),
            pltpu.VMEM((192, 192), BF16),
            pltpu.VMEM((6, 512, 512), F32),
            pltpu.VMEM((192, DEGREES), BF16),
            pltpu.VMEM((PEERS, 48, DEGREES), BF16),
            pltpu.VMEM((NQ, GX, 48, DEGREES), BF16),
            pltpu.VMEM((GX, 48, 128), BF16),
            pltpu.VMEM((NQ, GX, 48, 128), BF16),
            pltpu.VMEM((NZ, 2, 4, 128, 128), BF16),
            pltpu.VMEM((PAIRS, 256, DEGREES), BF16),
            pltpu.VMEM((256, 128), BF16),
            pltpu.VMEM((NQ, GX, 2, 2, 3, 16, 128), BF16),
            pltpu.VMEM((2, GX, 3, 16, 128), BF16),
            pltpu.VMEM((2, GX, 3, 16, 128), BF16),
            pltpu.VMEM((2, 2, 3, PEERS, 16, 128), BF16),
            pltpu.VMEM((2, 768, 512), BF16),
            pltpu.SemaphoreType.DMA,
            pltpu.SemaphoreType.DMA,
            pltpu.SemaphoreType.DMA((NQ, PAIRS, 2)),
            pltpu.SemaphoreType.DMA((2, 4)),
            pltpu.SemaphoreType.DMA((2, 4)),
            pltpu.SemaphoreType.DMA,
            pltpu.SemaphoreType.DMA((NQ // 2,)),
            pltpu.SemaphoreType.DMA,
            pltpu.SemaphoreType.DMA((NQ // 2,)),
            pltpu.SemaphoreType.DMA((2, 2, 4, 4)),
            pltpu.SemaphoreType.DMA((2, 2, 4, 4)),
            pltpu.SemaphoreType.DMA((2, 2)),
            pltpu.SemaphoreType.DMA((2, 2)),
            pltpu.SemaphoreType.DMA((2, 2)),
            pltpu.SemaphoreType.DMA((2, 2)),
            pltpu.SemaphoreType.DMA((2,)),
        ],
        compiler_params=pltpu.CompilerParams(
            collective_id=0, has_side_effects=True, vmem_limit_bytes=57 * 2**20
        ),
        cost_estimate=pl.CostEstimate(flops=2 * 10**9, bytes_accessed=10**7, transcendentals=0),
    )(counts, spectra, legendre, perm)


TILE = 256
STEPS = HALF // TILE
CHUNK = 16


def synthesis_kernel(field, geometry, left, table, out, factors, waves, stage, sems):
    squared = field[0]
    cos_theta = geometry[0]
    sin_theta = geometry[1]
    factors[0] = cos_theta
    factors[1] = sin_theta
    factors[2] = squared * cos_theta * sin_theta
    factors[3] = 0.5 * squared * sin_theta * sin_theta
    factors[4] = 2.0 * squared * cos_theta * cos_theta
    factors[5] = 0.5 * squared * (4.0 * cos_theta * cos_theta + sin_theta * sin_theta)

    def ship(i, h):
        return pltpu.make_async_copy(
            stage.at[i, h],
            out.at[0, :, :, pl.ds(h * HALF + i * TILE, TILE)],
            sems.at[i, h],
        )

    def wide(value):
        return jnp.concatenate([value] * (TILE // 128), axis=1)

    for i in range(STEPS):
        columns = pl.ds(i * TILE, TILE)
        for o in range(2):
            waves[i % 2, o] = jnp.dot(left[o], table[o, :, columns], preferred_element_type=F32)
        for r in range(0, NLAT_W, CHUNK):
            here = pl.ds(r, CHUNK)
            cos_w, sin_w, mix, own, twice, total = (wide(factors[n, here, :]) for n in range(6))
            even = [waves[i % 2, 0, pl.ds(128 * n + r, CHUNK), :] for n in range(6)]
            odd = [waves[i % 2, 1, pl.ds(128 * n + r, CHUNK), :] for n in range(6)]
            for h in range(2):
                flow = [a + b if h == 0 else a - b for a, b in zip(even, odd)]
                radial, polar, azimuth = flow[:3]
                stage[i, h, 0, here, :] = (
                    sin_w * azimuth + mix * polar - radial * (own + flow[3])
                ).astype(BF16)
                stage[i, h, 1, here, :] = (
                    cos_w * azimuth - twice * polar + radial * (mix - flow[4])
                ).astype(BF16)
                stage[i, h, 2, here, :] = (
                    -(cos_w * polar + total * azimuth + radial * (sin_w + flow[5]))
                ).astype(BF16)
        for h in range(2):
            ship(i, h).start()
    for i in range(STEPS):
        for h in range(2):
            ship(i, h).wait()


def synthesis(field, geometry, left, table):
    return pl.pallas_call(
        synthesis_kernel,
        out_shape=jax.ShapeDtypeStruct((1, 3, NLAT_W, LONGITUDE_COUNT), BF16),
        in_specs=[
            pl.BlockSpec(memory_space=pltpu.SMEM),
            pl.BlockSpec(memory_space=pltpu.VMEM),
            pl.BlockSpec(memory_space=pltpu.VMEM),
            pl.BlockSpec(memory_space=pltpu.VMEM),
        ],
        out_specs=pl.BlockSpec(memory_space=pl.ANY),
        scratch_shapes=[
            pltpu.VMEM((6, NLAT_W, 128), F32),
            pltpu.VMEM((2, 2, 768, TILE), F32),
            pltpu.VMEM((STEPS, 2, 3, NLAT_W, TILE), BF16),
            pltpu.SemaphoreType.DMA((STEPS, 2)),
        ],
        compiler_params=pltpu.CompilerParams(vmem_limit_bytes=32 * 2**20),
        cost_estimate=pl.CostEstimate(flops=3 * 10**9, bytes_accessed=7 * 10**6, transcendentals=0),
    )(field, geometry, left, table)


def shards(spectra, legendre, degree_counts):
    perm = jnp.asarray(order_permutation(), BF16)
    table = jnp.asarray(fourier_table(), BF16)
    theta = np.pi * (np.arange(NLAT_W) + (NLAT - NLAT_W) // 2 + 0.5) / NLAT
    geometry = np.repeat(np.stack([np.cos(theta), np.sin(theta)])[:, :, None], 128, axis=2)
    geometry = jnp.asarray(geometry, F32)
    shell = lax.axis_index(("grp", "sub")).astype(F32)
    radius = RADIUS_IN + (shell + 0.5) / SHELLS
    field = ((RADIUS_IN / radius) ** 6).reshape(1)
    left = exchange(degree_counts, spectra, legendre, perm)
    return synthesis(field, geometry, left, table)


def solution(mesh):
    in_specs = (P(("grp", "sub"), None, None, None), P("sub", None, None), P())
    out_specs = P(("grp", "sub"), None, None, None)
    return jax.shard_map(shards, mesh=mesh, in_specs=in_specs, out_specs=out_specs, check_vma=False)
```

```python
import math

import jax
import jax.numpy as jnp
import numpy as np
from jax import lax
from jax.experimental import pallas as pl
from jax.experimental.pallas import tpu as pltpu
from jax.sharding import PartitionSpec as P

MESH = pl.DeviceIdType.MESH
BF16 = jnp.bfloat16
F32 = jnp.float32

LOWEST_ORDER = 512
NLAT = 1536
NLAT_W = 128
LONGITUDE_COUNT = 3072
HALF = LONGITUDE_COUNT // 2
RADIUS_IN = 0.35 / 0.65
ELSASSER = 0.5
SHELLS = 256

GX, NZ, NQ = 4, 8, 8
PEERS = GX * NQ
PAIRS = NZ // 2
DEGREES = 512


def lanes_of(zb):
    return 512 - 128 * (zb // 2)


def order_permutation():
    p = np.zeros((192, 192), np.float32)
    for x in range(GX):
        for v in range(3):
            for o in range(2):
                for k in range(PAIRS):
                    for part in range(2):
                        p[x * 48 + v * 16 + o * 8 + k * 2 + part, k * 48 + (2 * v + part) * 8 + 2 * x + o] = 1
    return p


def fourier_table():
    x, q, h, k = np.meshgrid(np.arange(GX), np.arange(NQ), np.arange(2), np.arange(PAIRS), indexing="ij")
    block = 8 * k + q
    block = np.where(h == 0, block, np.where(block == 0, 32, 64 - block))
    first = (8 * block + 2 * x).reshape(-1)
    n = np.arange(HALF)
    out = np.zeros((2, first.size, 2, HALF), np.float32)
    for o in range(2):
        phase = ((LOWEST_ORDER + first + o)[:, None] * n[None, :]) % LONGITUDE_COUNT
        angle = phase * (2.0 * math.pi / LONGITUDE_COUNT)
        out[o, :, 0] = np.cos(angle)
        out[o, :, 1] = -np.sin(angle)
    return out.reshape(2, 2 * first.size, HALF)


def exchange_kernel(
    counts, spectra, legendre, perm, left,
    limits, mixer, rows, packed, sends, recv, sends_x, recv_x, basis, weights, weights_x, fd, low, high, field, turned,
    limit_sem, mixer_sem, rows_sem, own_send, own_recv, spec_send, spec_recv, x_send, x_recv, leg_send, leg_recv,
    end_send, end_recv, out_send, out_recv, left_sem,
):
    gx = lax.axis_index("grp")
    sub = lax.axis_index("sub")
    z, q = sub // NQ, sub % NQ
    me = gx * NQ + q
    y = q // 2
    up, down = (z + 1) % NZ, (z + NZ - 1) % NZ
    mirror = (NQ - q) % NQ
    column = jnp.where(z < PAIRS, q, mirror)

    def peer(x, qq):
        return (x, z * NQ + qq)

    def along(zz, qq):
        return (gx, zz * NQ + qq)

    barrier = pltpu.get_barrier_semaphore()

    @pl.loop(0, PEERS)
    def _(i):
        @pl.when(i != me)
        def _():
            pl.semaphore_signal(barrier, inc=1, device_id=peer(i // NQ, i % NQ), device_id_type=MESH)

    for zz in (up, down):
        for qq in (q, mirror):
            pl.semaphore_signal(barrier, inc=1, device_id=along(zz, qq), device_id_type=MESH)

    limit_copy = pltpu.make_async_copy(counts, limits, limit_sem)
    limit_copy.start()
    mixer_copy = pltpu.make_async_copy(perm, mixer, mixer_sem)
    mixer_copy.start()

    def pair_rows(k, qq):
        partner = 64 * (NZ - k) - 8 * qq
        if k == 0:
            partner = jnp.where(qq == 0, 256, partner)
        return pl.multiple_of(64 * k + 8 * qq, 8), pl.multiple_of(partner, 8)

    def row_copies(qq):
        copies = []
        for k in range(PAIRS):
            for h, (start, width) in enumerate(zip(pair_rows(k, qq), (lanes_of(k), 256))):
                copies.append(
                    pltpu.make_async_copy(
                        spectra.at[0, :, pl.ds(start, 8), pl.ds(0, width)],
                        rows.at[:, pl.ds(start, 8), pl.ds(0, width)],
                        rows_sem.at[qq, k, h],
                    )
                )
        return copies

    def place(i):
        return (y + i // 2) % (NQ // 2) * 2 + (q + i) % 2

    @pl.loop(0, NQ)
    def _(i):
        for copy in row_copies(place(i)):
            copy.start()

    def kept(start, width, valid):
        block = rows[:, pl.ds(start, 8), pl.ds(0, width)]
        order = lax.broadcasted_iota(jnp.int32, (8, width), 0) + start
        degree = lax.broadcasted_iota(jnp.int32, (8, width), 1)
        keep = degree < jnp.where(valid, jnp.maximum(limits[gx, 0] - order, 1), 0)
        return jnp.where(keep[None], block, 0.0).reshape(48, width)

    def pack(qq):
        for copy in row_copies(qq):
            copy.wait()
        for k in range(PAIRS):
            block = 8 * k + qq
            first, second = pair_rows(k, qq)
            width = lanes_of(k)
            one = kept(first, width, True)
            two = pltpu.roll(kept(second, 256, block > 0), (256 - 8 * block) % 256, 1)
            if width < DEGREES:
                one = jnp.concatenate([one, jnp.zeros((48, DEGREES - width), F32)], axis=1)
            both = jnp.concatenate([one[:, :256], one[:, 256:] + two], axis=1)
            packed[pl.ds(48 * k, 48), :] = both.astype(BF16)
        mixed = jnp.dot(mixer[...], packed[...], preferred_element_type=F32)
        sends[pl.ds(qq * GX, GX)] = mixed.astype(BF16).reshape(GX, 48, DEGREES)

        @pl.when(qq == 0)
        def _():
            alone = kept(256, 256, True).astype(BF16)
            zeros = jnp.zeros((96, 128), BF16)
            spread = jnp.concatenate([alone[:, :128], alone[:, 128:], zeros], axis=0)
            mixed = jnp.dot(mixer[...], spread, preferred_element_type=F32)
            sends_x[...] = mixed.astype(BF16).reshape(GX, 48, 128)

    def spec_copy(x, qq):
        return pltpu.make_async_remote_copy(
            src_ref=sends.at[qq * GX + x],
            dst_ref=recv.at[q, gx],
            send_sem=spec_send,
            recv_sem=spec_recv.at[y],
            device_id=peer(x, qq),
            device_id_type=MESH,
        )

    def spec_arrivals(yy):
        part = recv.at[pl.ds(2 * yy, 2)]
        return pltpu.make_async_copy(part, part, spec_recv.at[yy])

    def spec_departures():
        part = sends.at[pl.ds(0, PEERS - 1)]
        return pltpu.make_async_copy(part, part, spec_send)

    def x_copy(x):
        return pltpu.make_async_remote_copy(
            src_ref=sends_x.at[x],
            dst_ref=recv_x.at[q, gx],
            send_sem=x_send,
            recv_sem=x_recv.at[y],
            device_id=peer(x, 0),
            device_id_type=MESH,
        )

    def x_arrivals(yy):
        part = recv_x.at[pl.ds(2 * yy, 2)]
        return pltpu.make_async_copy(part, part, x_recv.at[yy])

    def x_departures(count):
        part = sends_x.at[pl.ds(0, count)]
        return pltpu.make_async_copy(part, part, x_send)

    def send_spec(qq):
        @pl.loop(0, GX)
        def _(j):
            x = (gx + j) % GX

            @pl.when(x * NQ + qq != me)
            def _():
                spec_copy(x, qq).start()

            @pl.when((x * NQ + qq != me) & (qq == 0))
            def _():
                x_copy(x).start()

    def pieces_of(zb):
        return 4 - zb // 2

    def mine_at(o, t):
        return legendre.at[2 * gx + o, :, pl.ds(128 * t, 128)]

    def leg_piece(o, step, way, t, arriving):
        shift = step + 1 if arriving else step
        zb = (z + NZ - shift) % NZ if way == 0 else (z + shift) % NZ
        onward, backward = (up, down) if way == 0 else (down, up)
        if arriving:
            target = along(backward, jnp.where(zb < PAIRS, q, mirror) if step == 0 else q)
        else:
            target = along(onward, column if step == 0 else q)
        copy = pltpu.make_async_remote_copy(
            src_ref=mine_at(o, t) if step == 0 and not arriving else basis.at[zb, o, t],
            dst_ref=basis.at[zb, o, t],
            send_sem=leg_send.at[o, way, step, t],
            recv_sem=leg_recv.at[o, way, step, t],
            device_id=target,
            device_id_type=MESH,
        )
        return t < pieces_of(zb), copy

    def goes(step, way, t):
        return step < 3 or way == t % 2

    def own_remote(o, t):
        return pltpu.make_async_remote_copy(
            src_ref=mine_at(o, t),
            dst_ref=basis.at[z, o, t],
            send_sem=own_send.at[o, t],
            recv_sem=own_recv.at[o, t],
            device_id=along(z, mirror),
            device_id_type=MESH,
        )

    def own_local(o, t):
        return pltpu.make_async_copy(mine_at(o, t), basis.at[z, o, t], own_recv.at[o, t])

    def own_each(o, remote, local):
        for t in range(4):
            here = t < pieces_of(z)

            @pl.when(here & (column != q))
            def _():
                remote(own_remote(o, t))

            if local is None:
                continue

            @pl.when(here & (column == q))
            def _():
                local(own_local(o, t))

    def leg_first(o):
        for t in range(4):
            for way in range(2):
                here, copy = leg_piece(o, 0, way, t, False)
                pl.when(here)(copy.start)
        own_each(o, lambda c: c.start(), lambda c: c.start())

    def leg_forward(o, step):
        for way in range(2):
            for t in range(4):
                if not goes(step, way, t):
                    continue
                here, arrival = leg_piece(o, step, way, t, True)

                @pl.when(here)
                def _():
                    arrival.wait_recv()
                    if step < 3 and goes(step + 1, way, t):
                        leg_piece(o, step + 1, way, t, False)[1].start()

    limit_copy.wait()
    mixer_copy.wait()
    pack(q)
    pl.semaphore_wait(barrier, PEERS - 1 + 4)
    leg_first(0)
    send_spec(q)
    pltpu.make_async_copy(sends.at[q * GX + gx], recv.at[q, gx], spec_recv.at[y]).start()

    @pl.when(q == 0)
    def _():
        pltpu.make_async_copy(sends_x.at[gx], recv_x.at[0, gx], x_recv.at[0]).start()

    @pl.when(q != 0)
    def _():
        recv_x[...] = jnp.zeros_like(recv_x)

    def pack_and_send(i):
        pack(place(i))
        send_spec(place(i))

    leg_first(1)
    pl.loop(1, 8)(pack_and_send)
    leg_forward(0, 0)
    leg_forward(1, 0)
    leg_forward(0, 1)
    leg_forward(1, 1)
    leg_forward(0, 2)
    leg_forward(1, 2)
    leg_forward(0, 3)
    own_each(0, lambda c: c.wait_recv(), lambda c: c.wait())

    def out_copy(x, qq, what, o):
        return pltpu.make_async_remote_copy(
            src_ref=fd.at[qq, x, what, o],
            dst_ref=field.at[what, o, me],
            send_sem=out_send.at[what, o],
            recv_sem=out_recv.at[what, o],
            device_id=peer(x, qq),
            device_id_type=MESH,
        )

    def out_arrivals(what, o):
        part = field.at[what, o]
        return pltpu.make_async_copy(part, part, out_recv.at[what, o])

    def out_departures(what, o):
        part = field.at[what, o, pl.ds(0, PEERS - 1)]
        return pltpu.make_async_copy(part, part, out_send.at[what, o])

    def send_out(qq, what, o):
        @pl.loop(0, GX)
        def _(j):
            x = (gx + j) % GX

            @pl.when(x * NQ + qq != me)
            def _():
                out_copy(x, qq, what, o).start()

        @pl.when(qq == q)
        def _():
            pltpu.make_async_copy(
                fd.at[q, gx, what, o], field.at[what, o, me], out_recv.at[what, o]
            ).start()

    def low_copy(o):
        return pltpu.make_async_remote_copy(
            src_ref=fd.at[NQ - 1, :, 0, o],
            dst_ref=low.at[o],
            send_sem=end_send.at[0, o],
            recv_sem=end_recv.at[0, o],
            device_id=along(up, q),
            device_id_type=MESH,
        )

    def high_copy(o):
        return pltpu.make_async_remote_copy(
            src_ref=fd.at[0, :, 0, o],
            dst_ref=high.at[o],
            send_sem=end_send.at[1, o],
            recv_sem=end_recv.at[1, o],
            device_id=along(down, q),
            device_id_type=MESH,
        )

    rows384 = lax.broadcasted_iota(jnp.int32, (384, 256), 0)
    pair_of = rows384 % 8 // 2

    def inner_differences(yy, o):
        @pl.when(yy < NQ // 2 - 1)
        def _():
            m = 2 * yy + 1
            outer = fd[pl.ds(m + 1, 2), :, 0, o].astype(F32)
            inner = fd[pl.ds(m - 1, 2), :, 0, o].astype(F32)
            fd[pl.ds(m, 2), :, 1, o] = (0.5 * (outer - inner)).astype(BF16)
            send_out(m, 1, o)
            send_out(m + 1, 1, o)

    def end_differences(o):
        low_copy(o).wait_recv()
        high_copy(o).wait_recv()
        for x in range(GX):
            bottom = fd[0, x, 0, o].astype(F32)
            second = fd[1, x, 0, o].astype(F32)
            before = low[o, x - 1].astype(F32) if x > 0 else 2.0 * bottom - second
            below = jnp.where(z == 0, before, low[o, x].astype(F32))
            fd[0, x, 1, o] = (0.5 * (second - below)).astype(BF16)
            top = fd[NQ - 1, x, 0, o].astype(F32)
            last = fd[NQ - 2, x, 0, o].astype(F32)
            after = high[o, x + 1].astype(F32) if x < GX - 1 else 2.0 * top - last
            above = jnp.where(z == NZ - 1, after, high[o, x].astype(F32))
            fd[NQ - 1, x, 1, o] = (0.5 * (above - last)).astype(BF16)
        send_out(0, 1, o)
        send_out(NQ - 1, 1, o)

    def build_weights(o):
        lane = lax.broadcasted_iota(jnp.int32, (128, DEGREES), 1)
        for k in range(PAIRS):
            block = 8 * k + q
            cut = DEGREES - 8 * block
            one = jnp.concatenate([basis[k, o, t] for t in range(4)], axis=1).astype(F32)
            weights[k, 0:128, :] = jnp.where(lane < cut, one, 0.0).astype(BF16)
            zb = jnp.where(q == 0, NZ - max(k, 1), NZ - 1 - k)
            two = jnp.concatenate([basis[zb, o, t] for t in range(2)], axis=1).astype(F32)
            two = pltpu.roll(two, (256 - 8 * block) % 256, 1)
            two = jnp.where(lane[:, 256:] >= cut, two, 0.0)
            weights[k, 128:256, :] = jnp.concatenate([jnp.zeros((128, 256), F32), two], axis=1).astype(BF16)
        weights_x[...] = jnp.concatenate([basis[PAIRS, o, t] for t in range(2)], axis=0)

    def coefficients(o):
        @pl.loop(0, NQ // 2)
        def _(i):
            yy = (y + NQ // 2 - i) % (NQ // 2)
            two = pl.ds(2 * yy, 2)
            if o == 0:
                spec_arrivals(yy).wait()

                @pl.when(q == 0)
                def _():
                    x_arrivals(yy).wait()

            if o == 1:
                @pl.when(i == 2)
                def _():
                    end_differences(0)

            block = recv[two].reshape(384, DEGREES)
            total = jnp.zeros((384, 256), F32)
            for k in range(PAIRS):
                both = lax.dot_general(block, weights[k], (((1,), (1,)), ((), ())), preferred_element_type=F32)
                total = jnp.where(pair_of == k, both, total)
            extra = lax.dot_general(
                recv_x[two].reshape(384, 128), weights_x[...], (((1,), (1,)), ((), ())), preferred_element_type=F32
            )
            extra = extra[:, :128] + pltpu.roll(extra[:, 128:], 382, 0)
            lower = total[:, :128]
            upper = total[:, 128:] + jnp.where(pair_of[:, :128] == 0, extra, 0.0)
            both = [part.reshape(2, GX, 3, 2, 8, 128)[:, :, :, o] for part in (lower, upper)]
            fd[two, :, 0, o] = jnp.concatenate(both, axis=3).astype(BF16)
            send_out(2 * yy, 0, o)
            send_out(2 * yy + 1, 0, o)

            @pl.when(yy == NQ // 2 - 1)
            def _():
                low_copy(o).start()

            @pl.when(yy == 0)
            def _():
                high_copy(o).start()

            @pl.when(i >= 1)
            def _():
                inner_differences(yy, o)

        inner_differences(y, o)

    build_weights(0)
    coefficients(0)
    leg_forward(1, 3)
    own_each(1, lambda c: c.wait_recv(), lambda c: c.wait())
    build_weights(1)
    coefficients(1)
    end_differences(1)

    def left_copy(o):
        return pltpu.make_async_copy(turned.at[o], left.at[o], left_sem.at[o])

    spec_departures().wait()

    @pl.when(q == 0)
    def _():
        x_departures(GX - 1).wait()

    @pl.when(q != 0)
    def _():
        x_departures(GX).wait()

    for o in range(2):
        low_copy(o).wait_send()
        high_copy(o).wait_send()
        own_each(o, lambda c: c.wait_send(), None)
        for step in range(4):
            for t in range(4):
                for way in range(2):
                    if goes(step, way, t):
                        here, copy = leg_piece(o, step, way, t, False)
                        pl.when(here)(copy.wait_send)

    for o in range(2):
        for what in range(2):
            out_arrivals(what, o).wait()
            for v in range(3):
                block = field[what, o, :, v].reshape(512, 128)
                turned[o, pl.ds(128 * (3 * what + v), 128), :] = block.T
        left_copy(o).start()

    for o in range(2):
        for what in range(2):
            out_departures(what, o).wait()
        left_copy(o).wait()


def exchange(counts, spectra, legendre, perm):
    return pl.pallas_call(
        exchange_kernel,
        out_shape=jax.ShapeDtypeStruct((2, 768, 512), BF16),
        in_specs=[pl.BlockSpec(memory_space=pl.ANY)] * 4,
        out_specs=pl.BlockSpec(memory_space=pl.ANY),
        scratch_shapes=[
            pltpu.SMEM((GX, 512), jnp.int32),
            pltpu.VMEM((192, 192), BF16),
            pltpu.VMEM((6, 512, 512), F32),
            pltpu.VMEM((192, DEGREES), BF16),
            pltpu.VMEM((PEERS, 48, DEGREES), BF16),
            pltpu.VMEM((NQ, GX, 48, DEGREES), BF16),
            pltpu.VMEM((GX, 48, 128), BF16),
            pltpu.VMEM((NQ, GX, 48, 128), BF16),
            pltpu.VMEM((NZ, 2, 4, 128, 128), BF16),
            pltpu.VMEM((PAIRS, 256, DEGREES), BF16),
            pltpu.VMEM((256, 128), BF16),
            pltpu.VMEM((NQ, GX, 2, 2, 3, 16, 128), BF16),
            pltpu.VMEM((2, GX, 3, 16, 128), BF16),
            pltpu.VMEM((2, GX, 3, 16, 128), BF16),
            pltpu.VMEM((2, 2, PEERS, 3, 16, 128), BF16),
            pltpu.VMEM((2, 768, 512), BF16),
            pltpu.SemaphoreType.DMA,
            pltpu.SemaphoreType.DMA,
            pltpu.SemaphoreType.DMA((NQ, PAIRS, 2)),
            pltpu.SemaphoreType.DMA((2, 4)),
            pltpu.SemaphoreType.DMA((2, 4)),
            pltpu.SemaphoreType.DMA,
            pltpu.SemaphoreType.DMA((NQ // 2,)),
            pltpu.SemaphoreType.DMA,
            pltpu.SemaphoreType.DMA((NQ // 2,)),
            pltpu.SemaphoreType.DMA((2, 2, 4, 4)),
            pltpu.SemaphoreType.DMA((2, 2, 4, 4)),
            pltpu.SemaphoreType.DMA((2, 2)),
            pltpu.SemaphoreType.DMA((2, 2)),
            pltpu.SemaphoreType.DMA((2, 2)),
            pltpu.SemaphoreType.DMA((2, 2)),
            pltpu.SemaphoreType.DMA((2,)),
        ],
        compiler_params=pltpu.CompilerParams(
            collective_id=0, has_side_effects=True, vmem_limit_bytes=32 * 2**20
        ),
        cost_estimate=pl.CostEstimate(flops=2 * 10**9, bytes_accessed=10**7, transcendentals=0),
    )(*(pltpu.with_memory_space_constraint(a, pltpu.HBM) for a in (counts, spectra, legendre, perm)))


TILE = 256
STEPS = HALF // TILE
CHUNK = 16


def synthesis_kernel(field, geometry, left, table, out, factors, waves, stage, sems):
    squared = field[0]
    cos_theta = geometry[0]
    sin_theta = geometry[1]
    factors[0] = cos_theta
    factors[1] = sin_theta
    factors[2] = squared * cos_theta * sin_theta
    factors[3] = 0.5 * squared * sin_theta * sin_theta
    factors[4] = 2.0 * squared * cos_theta * cos_theta
    factors[5] = 0.5 * squared * (4.0 * cos_theta * cos_theta + sin_theta * sin_theta)

    def ship(i, h):
        return pltpu.make_async_copy(
            stage.at[i, h],
            out.at[0, :, :, pl.ds(h * HALF + i * TILE, TILE)],
            sems.at[i, h],
        )

    def wide(value):
        return jnp.concatenate([value] * (TILE // 128), axis=1)

    for i in range(STEPS):
        columns = pl.ds(i * TILE, TILE)
        for o in range(2):
            waves[i % 2, o] = jnp.dot(left[o], table[o, :, columns], preferred_element_type=F32)
        for r in range(0, NLAT_W, CHUNK):
            here = pl.ds(r, CHUNK)
            cos_w, sin_w, mix, own, twice, total = (wide(factors[n, here, :]) for n in range(6))
            even = [waves[i % 2, 0, pl.ds(128 * n + r, CHUNK), :] for n in range(6)]
            odd = [waves[i % 2, 1, pl.ds(128 * n + r, CHUNK), :] for n in range(6)]
            for h in range(2):
                flow = [a + b if h == 0 else a - b for a, b in zip(even, odd)]
                radial, polar, azimuth = flow[:3]
                stage[i, h, 0, here, :] = (
                    sin_w * azimuth + mix * polar - radial * (own + flow[3])
                ).astype(BF16)
                stage[i, h, 1, here, :] = (
                    cos_w * azimuth - twice * polar + radial * (mix - flow[4])
                ).astype(BF16)
                stage[i, h, 2, here, :] = (
                    -(cos_w * polar + total * azimuth + radial * (sin_w + flow[5]))
                ).astype(BF16)
        for h in range(2):
            ship(i, h).start()
    for i in range(STEPS):
        for h in range(2):
            ship(i, h).wait()


def synthesis(field, geometry, left, table):
    return pl.pallas_call(
        synthesis_kernel,
        out_shape=jax.ShapeDtypeStruct((1, 3, NLAT_W, LONGITUDE_COUNT), BF16),
        in_specs=[
            pl.BlockSpec(memory_space=pltpu.SMEM),
            pl.BlockSpec(memory_space=pltpu.VMEM),
            pl.BlockSpec(memory_space=pltpu.VMEM),
            pl.BlockSpec(memory_space=pltpu.VMEM),
        ],
        out_specs=pl.BlockSpec(memory_space=pl.ANY),
        scratch_shapes=[
            pltpu.VMEM((6, NLAT_W, 128), F32),
            pltpu.VMEM((2, 2, 768, TILE), F32),
            pltpu.VMEM((STEPS, 2, 3, NLAT_W, TILE), BF16),
            pltpu.SemaphoreType.DMA((STEPS, 2)),
        ],
        compiler_params=pltpu.CompilerParams(vmem_limit_bytes=32 * 2**20),
        cost_estimate=pl.CostEstimate(flops=3 * 10**9, bytes_accessed=7 * 10**6, transcendentals=0),
    )(field, geometry, left, table)


def shards(spectra, legendre, degree_counts):
    perm = jnp.asarray(order_permutation(), BF16)
    table = jnp.asarray(fourier_table(), BF16)
    theta = np.pi * (np.arange(NLAT_W) + (NLAT - NLAT_W) // 2 + 0.5) / NLAT
    geometry = np.repeat(np.stack([np.cos(theta), np.sin(theta)])[:, :, None], 128, axis=2)
    geometry = jnp.asarray(geometry, F32)
    shell = lax.axis_index(("grp", "sub")).astype(F32)
    radius = RADIUS_IN + (shell + 0.5) / SHELLS
    field = ((RADIUS_IN / radius) ** 6).reshape(1)
    left = exchange(degree_counts, spectra, legendre, perm)
    return synthesis(field, geometry, left, table)


def solution(mesh):
    in_specs = (P(("grp", "sub"), None, None, None), P("sub", None, None), P())
    out_specs = P(("grp", "sub"), None, None, None)
    return jax.shard_map(shards, mesh=mesh, in_specs=in_specs, out_specs=out_specs, check_vma=False)
```

```python
import math

import jax
import jax.numpy as jnp
import numpy as np
from jax import lax
from jax.experimental import pallas as pl
from jax.experimental.pallas import tpu as pltpu
from jax.sharding import PartitionSpec as P

MESH = pl.DeviceIdType.MESH
BF16 = jnp.bfloat16
F32 = jnp.float32

LOWEST_ORDER = 512
NLAT = 1536
NLAT_W = 128
LONGITUDE_COUNT = 3072
HALF = LONGITUDE_COUNT // 2
RADIUS_IN = 0.35 / 0.65
ELSASSER = 0.5
SHELLS = 256

GX, NZ, NQ = 4, 8, 8
PEERS = GX * NQ
PAIRS = NZ // 2
DEGREES = 512


def lanes_of(zb):
    return 512 - 128 * (zb // 2)


def order_permutation():
    p = np.zeros((192, 192), np.float32)
    for x in range(GX):
        for v in range(3):
            for o in range(2):
                for k in range(PAIRS):
                    for part in range(2):
                        p[x * 48 + v * 16 + o * 8 + k * 2 + part, k * 48 + (2 * v + part) * 8 + 2 * x + o] = 1
    return p


def fourier_table():
    x, q, h, k = np.meshgrid(np.arange(GX), np.arange(NQ), np.arange(2), np.arange(PAIRS), indexing="ij")
    block = 8 * k + q
    block = np.where(h == 0, block, np.where(block == 0, 32, 64 - block))
    first = (8 * block + 2 * x).reshape(-1)
    n = np.arange(HALF)
    out = np.zeros((2, first.size, 2, HALF), np.float32)
    for o in range(2):
        phase = ((LOWEST_ORDER + first + o)[:, None] * n[None, :]) % LONGITUDE_COUNT
        angle = phase * (2.0 * math.pi / LONGITUDE_COUNT)
        out[o, :, 0] = np.cos(angle)
        out[o, :, 1] = -np.sin(angle)
    return out.reshape(2, 2 * first.size, HALF)


def exchange_kernel(
    counts, spectra, legendre, perm, left,
    limits, mixer, rows, packed, sends, recv, sends_x, recv_x, basis, weights, weights_x, fd, low, high, field, turned,
    limit_sem, mixer_sem, rows_sem, own_send, own_recv, spec_send, spec_recv, x_send, x_recv, leg_send, leg_recv,
    end_send, end_recv, out_send, out_recv, left_sem,
):
    gx = lax.axis_index("grp")
    sub = lax.axis_index("sub")
    z, q = sub // NQ, sub % NQ
    me = gx * NQ + q
    y = q // 2
    up, down = (z + 1) % NZ, (z + NZ - 1) % NZ
    mirror = (NQ - q) % NQ
    column = jnp.where(z < PAIRS, q, mirror)

    def peer(x, qq):
        return (x, z * NQ + qq)

    def along(zz, qq):
        return (gx, zz * NQ + qq)

    barrier = pltpu.get_barrier_semaphore()

    @pl.loop(0, PEERS)
    def _(i):
        @pl.when(i != me)
        def _():
            pl.semaphore_signal(barrier, inc=1, device_id=peer(i // NQ, i % NQ), device_id_type=MESH)

    for zz in (up, down):
        for qq in (q, mirror):
            pl.semaphore_signal(barrier, inc=1, device_id=along(zz, qq), device_id_type=MESH)

    limit_copy = pltpu.make_async_copy(counts, limits, limit_sem)
    limit_copy.start()
    mixer_copy = pltpu.make_async_copy(perm, mixer, mixer_sem)
    mixer_copy.start()

    def pair_rows(k, qq):
        partner = 64 * (NZ - k) - 8 * qq
        if k == 0:
            partner = jnp.where(qq == 0, 256, partner)
        return pl.multiple_of(64 * k + 8 * qq, 8), pl.multiple_of(partner, 8)

    def row_copies(qq):
        copies = []
        for k in range(PAIRS):
            for h, (start, width) in enumerate(zip(pair_rows(k, qq), (lanes_of(k), 256))):
                copies.append(
                    pltpu.make_async_copy(
                        spectra.at[0, :, pl.ds(start, 8), pl.ds(0, width)],
                        rows.at[:, pl.ds(start, 8), pl.ds(0, width)],
                        rows_sem.at[qq, k, h],
                    )
                )
        return copies

    def place(i):
        return (y + i // 2) % (NQ // 2) * 2 + (q + i) % 2

    @pl.loop(0, NQ)
    def _(i):
        for copy in row_copies(place(i)):
            copy.start()

    def kept(start, width, valid):
        block = rows[:, pl.ds(start, 8), pl.ds(0, width)]
        order = lax.broadcasted_iota(jnp.int32, (8, width), 0) + start
        degree = lax.broadcasted_iota(jnp.int32, (8, width), 1)
        keep = degree < jnp.where(valid, jnp.maximum(limits[gx, 0] - order, 1), 0)
        return jnp.where(keep[None], block, 0.0).reshape(48, width)

    def pack(qq):
        for copy in row_copies(qq):
            copy.wait()
        for k in range(PAIRS):
            block = 8 * k + qq
            first, second = pair_rows(k, qq)
            width = lanes_of(k)
            one = kept(first, width, True)
            two = pltpu.roll(kept(second, 256, block > 0), (256 - 8 * block) % 256, 1)
            if width < DEGREES:
                one = jnp.concatenate([one, jnp.zeros((48, DEGREES - width), F32)], axis=1)
            both = jnp.concatenate([one[:, :256], one[:, 256:] + two], axis=1)
            packed[pl.ds(48 * k, 48), :] = both.astype(BF16)
        mixed = jnp.dot(mixer[...], packed[...], preferred_element_type=F32)
        sends[pl.ds(qq * GX, GX)] = mixed.astype(BF16).reshape(GX, 48, DEGREES)

        @pl.when(qq == 0)
        def _():
            alone = kept(256, 256, True).astype(BF16)
            zeros = jnp.zeros((96, 128), BF16)
            spread = jnp.concatenate([alone[:, :128], alone[:, 128:], zeros], axis=0)
            mixed = jnp.dot(mixer[...], spread, preferred_element_type=F32)
            sends_x[...] = mixed.astype(BF16).reshape(GX, 48, 128)

    def spec_copy(x, qq):
        return pltpu.make_async_remote_copy(
            src_ref=sends.at[qq * GX + x],
            dst_ref=recv.at[q, gx],
            send_sem=spec_send,
            recv_sem=spec_recv.at[y],
            device_id=peer(x, qq),
            device_id_type=MESH,
        )

    def spec_arrivals(yy):
        part = recv.at[pl.ds(2 * yy, 2)]
        return pltpu.make_async_copy(part, part, spec_recv.at[yy])

    def spec_departures():
        part = sends.at[pl.ds(0, PEERS - 1)]
        return pltpu.make_async_copy(part, part, spec_send)

    def x_copy(x):
        return pltpu.make_async_remote_copy(
            src_ref=sends_x.at[x],
            dst_ref=recv_x.at[q, gx],
            send_sem=x_send,
            recv_sem=x_recv.at[y],
            device_id=peer(x, 0),
            device_id_type=MESH,
        )

    def x_arrivals(yy):
        part = recv_x.at[pl.ds(2 * yy, 2)]
        return pltpu.make_async_copy(part, part, x_recv.at[yy])

    def x_departures(count):
        part = sends_x.at[pl.ds(0, count)]
        return pltpu.make_async_copy(part, part, x_send)

    def send_spec(qq):
        @pl.loop(0, GX)
        def _(j):
            x = (gx + j + q) % GX

            @pl.when(x * NQ + qq != me)
            def _():
                spec_copy(x, qq).start()

            @pl.when((x * NQ + qq != me) & (qq == 0))
            def _():
                x_copy(x).start()

    def pieces_of(zb):
        return 4 - zb // 2

    def mine_at(o, t):
        return legendre.at[2 * gx + o, :, pl.ds(128 * t, 128)]

    def leg_piece(o, step, way, t, arriving):
        shift = step + 1 if arriving else step
        zb = (z + NZ - shift) % NZ if way == 0 else (z + shift) % NZ
        onward, backward = (up, down) if way == 0 else (down, up)
        if arriving:
            target = along(backward, jnp.where(zb < PAIRS, q, mirror) if step == 0 else q)
        else:
            target = along(onward, column if step == 0 else q)
        copy = pltpu.make_async_remote_copy(
            src_ref=mine_at(o, t) if step == 0 and not arriving else basis.at[zb, o, t],
            dst_ref=basis.at[zb, o, t],
            send_sem=leg_send.at[o, way, step, t],
            recv_sem=leg_recv.at[o, way, step, t],
            device_id=target,
            device_id_type=MESH,
        )
        return t < pieces_of(zb), copy

    def goes(step, way, t):
        return step < 3 or way == t % 2

    def own_remote(o, t):
        return pltpu.make_async_remote_copy(
            src_ref=mine_at(o, t),
            dst_ref=basis.at[z, o, t],
            send_sem=own_send.at[o, t],
            recv_sem=own_recv.at[o, t],
            device_id=along(z, mirror),
            device_id_type=MESH,
        )

    def own_local(o, t):
        return pltpu.make_async_copy(mine_at(o, t), basis.at[z, o, t], own_recv.at[o, t])

    def own_each(o, remote, local):
        for t in range(4):
            here = t < pieces_of(z)

            @pl.when(here & (column != q))
            def _():
                remote(own_remote(o, t))

            if local is None:
                continue

            @pl.when(here & (column == q))
            def _():
                local(own_local(o, t))

    def leg_first(o):
        for t in range(4):
            for way in range(2):
                here, copy = leg_piece(o, 0, way, t, False)
                pl.when(here)(copy.start)
        own_each(o, lambda c: c.start(), lambda c: c.start())

    def leg_forward(o, step):
        for way in range(2):
            for t in range(4):
                if not goes(step, way, t):
                    continue
                here, arrival = leg_piece(o, step, way, t, True)

                @pl.when(here)
                def _():
                    arrival.wait_recv()
                    if step < 3 and goes(step + 1, way, t):
                        leg_piece(o, step + 1, way, t, False)[1].start()

    limit_copy.wait()
    mixer_copy.wait()
    pack(q)
    pl.semaphore_wait(barrier, PEERS - 1 + 4)
    leg_first(0)
    send_spec(q)
    pltpu.make_async_copy(sends.at[q * GX + gx], recv.at[q, gx], spec_recv.at[y]).start()

    @pl.when(q == 0)
    def _():
        pltpu.make_async_copy(sends_x.at[gx], recv_x.at[0, gx], x_recv.at[0]).start()

    @pl.when(q != 0)
    def _():
        recv_x[...] = jnp.zeros_like(recv_x)

    def pack_and_send(i):
        pack(place(i))
        send_spec(place(i))

    pl.loop(1, 8)(pack_and_send)
    leg_first(1)
    leg_forward(0, 0)
    leg_forward(1, 0)
    leg_forward(0, 1)
    leg_forward(1, 1)
    leg_forward(0, 2)
    leg_forward(1, 2)
    leg_forward(0, 3)
    own_each(0, lambda c: c.wait_recv(), lambda c: c.wait())

    def out_copy(x, qq, what, o):
        return pltpu.make_async_remote_copy(
            src_ref=fd.at[qq, x, what, o],
            dst_ref=field.at[what, o, me],
            send_sem=out_send.at[what, o],
            recv_sem=out_recv.at[what, o],
            device_id=peer(x, qq),
            device_id_type=MESH,
        )

    def out_arrivals(what, o):
        part = field.at[what, o]
        return pltpu.make_async_copy(part, part, out_recv.at[what, o])

    def out_departures(what, o):
        part = field.at[what, o, pl.ds(0, PEERS - 1)]
        return pltpu.make_async_copy(part, part, out_send.at[what, o])

    def send_out(qq, what, o):
        @pl.loop(0, GX)
        def _(j):
            x = (gx + j + q) % GX

            @pl.when(x * NQ + qq != me)
            def _():
                out_copy(x, qq, what, o).start()

        @pl.when(qq == q)
        def _():
            pltpu.make_async_copy(
                fd.at[q, gx, what, o], field.at[what, o, me], out_recv.at[what, o]
            ).start()

    def low_copy(o):
        return pltpu.make_async_remote_copy(
            src_ref=fd.at[NQ - 1, :, 0, o],
            dst_ref=low.at[o],
            send_sem=end_send.at[0, o],
            recv_sem=end_recv.at[0, o],
            device_id=along(up, q),
            device_id_type=MESH,
        )

    def high_copy(o):
        return pltpu.make_async_remote_copy(
            src_ref=fd.at[0, :, 0, o],
            dst_ref=high.at[o],
            send_sem=end_send.at[1, o],
            recv_sem=end_recv.at[1, o],
            device_id=along(down, q),
            device_id_type=MESH,
        )

    rows384 = lax.broadcasted_iota(jnp.int32, (384, 256), 0)
    pair_of = rows384 % 8 // 2

    def inner_differences(yy, o):
        @pl.when(yy < NQ // 2 - 1)
        def _():
            m = 2 * yy + 1
            outer = fd[pl.ds(m + 1, 2), :, 0, o].astype(F32)
            inner = fd[pl.ds(m - 1, 2), :, 0, o].astype(F32)
            fd[pl.ds(m, 2), :, 1, o] = (0.5 * (outer - inner)).astype(BF16)
            send_out(m, 1, o)
            send_out(m + 1, 1, o)

    def end_differences(o):
        low_copy(o).wait_recv()
        high_copy(o).wait_recv()
        for x in range(GX):
            bottom = fd[0, x, 0, o].astype(F32)
            second = fd[1, x, 0, o].astype(F32)
            before = low[o, x - 1].astype(F32) if x > 0 else 2.0 * bottom - second
            below = jnp.where(z == 0, before, low[o, x].astype(F32))
            fd[0, x, 1, o] = (0.5 * (second - below)).astype(BF16)
            top = fd[NQ - 1, x, 0, o].astype(F32)
            last = fd[NQ - 2, x, 0, o].astype(F32)
            after = high[o, x + 1].astype(F32) if x < GX - 1 else 2.0 * top - last
            above = jnp.where(z == NZ - 1, after, high[o, x].astype(F32))
            fd[NQ - 1, x, 1, o] = (0.5 * (above - last)).astype(BF16)
        send_out(0, 1, o)
        send_out(NQ - 1, 1, o)

    def build_weights(o):
        lane = lax.broadcasted_iota(jnp.int32, (128, DEGREES), 1)
        for k in range(PAIRS):
            block = 8 * k + q
            cut = DEGREES - 8 * block
            one = jnp.concatenate([basis[k, o, t] for t in range(4)], axis=1).astype(F32)
            weights[k, 0:128, :] = jnp.where(lane < cut, one, 0.0).astype(BF16)
            zb = jnp.where(q == 0, NZ - max(k, 1), NZ - 1 - k)
            two = jnp.concatenate([basis[zb, o, t] for t in range(2)], axis=1).astype(F32)
            two = pltpu.roll(two, (256 - 8 * block) % 256, 1)
            two = jnp.where(lane[:, 256:] >= cut, two, 0.0)
            weights[k, 128:256, :] = jnp.concatenate([jnp.zeros((128, 256), F32), two], axis=1).astype(BF16)
        weights_x[...] = jnp.concatenate([basis[PAIRS, o, t] for t in range(2)], axis=0)

    def coefficients(o):
        @pl.loop(0, NQ // 2)
        def _(i):
            yy = (y + NQ // 2 - i) % (NQ // 2)
            two = pl.ds(2 * yy, 2)
            if o == 0:
                spec_arrivals(yy).wait()

                @pl.when(q == 0)
                def _():
                    x_arrivals(yy).wait()

            if o == 1:
                @pl.when(i == 2)
                def _():
                    end_differences(0)

            block = recv[two].reshape(384, DEGREES)
            total = jnp.zeros((384, 256), F32)
            for k in range(PAIRS):
                both = lax.dot_general(block, weights[k], (((1,), (1,)), ((), ())), preferred_element_type=F32)
                total = jnp.where(pair_of == k, both, total)
            extra = lax.dot_general(
                recv_x[two].reshape(384, 128), weights_x[...], (((1,), (1,)), ((), ())), preferred_element_type=F32
            )
            extra = extra[:, :128] + pltpu.roll(extra[:, 128:], 382, 0)
            lower = total[:, :128]
            upper = total[:, 128:] + jnp.where(pair_of[:, :128] == 0, extra, 0.0)
            both = [part.reshape(2, GX, 3, 2, 8, 128)[:, :, :, o] for part in (lower, upper)]
            fd[two, :, 0, o] = jnp.concatenate(both, axis=3).astype(BF16)
            send_out(2 * yy, 0, o)
            send_out(2 * yy + 1, 0, o)

            @pl.when(yy == NQ // 2 - 1)
            def _():
                low_copy(o).start()

            @pl.when(yy == 0)
            def _():
                high_copy(o).start()

            @pl.when(i >= 1)
            def _():
                inner_differences(yy, o)

        inner_differences(y, o)

    build_weights(0)
    coefficients(0)
    leg_forward(1, 3)
    own_each(1, lambda c: c.wait_recv(), lambda c: c.wait())
    build_weights(1)
    coefficients(1)
    end_differences(1)

    def left_copy(o):
        return pltpu.make_async_copy(turned.at[o], left.at[o], left_sem.at[o])

    spec_departures().wait()

    @pl.when(q == 0)
    def _():
        x_departures(GX - 1).wait()

    @pl.when(q != 0)
    def _():
        x_departures(GX).wait()

    for o in range(2):
        low_copy(o).wait_send()
        high_copy(o).wait_send()
        own_each(o, lambda c: c.wait_send(), None)
        for step in range(4):
            for t in range(4):
                for way in range(2):
                    if goes(step, way, t):
                        here, copy = leg_piece(o, step, way, t, False)
                        pl.when(here)(copy.wait_send)

    for o in range(2):
        for what in range(2):
            out_arrivals(what, o).wait()
            for v in range(3):
                block = field[what, o, :, v].reshape(512, 128)
                turned[o, pl.ds(128 * (3 * what + v), 128), :] = block.T
        left_copy(o).start()

    for o in range(2):
        for what in range(2):
            out_departures(what, o).wait()
        left_copy(o).wait()


def exchange(counts, spectra, legendre, perm):
    return pl.pallas_call(
        exchange_kernel,
        out_shape=jax.ShapeDtypeStruct((2, 768, 512), BF16),
        in_specs=[pl.BlockSpec(memory_space=pl.ANY)] * 4,
        out_specs=pl.BlockSpec(memory_space=pl.ANY),
        scratch_shapes=[
            pltpu.SMEM((GX, 512), jnp.int32),
            pltpu.VMEM((192, 192), BF16),
            pltpu.VMEM((6, 512, 512), F32),
            pltpu.VMEM((192, DEGREES), BF16),
            pltpu.VMEM((PEERS, 48, DEGREES), BF16),
            pltpu.VMEM((NQ, GX, 48, DEGREES), BF16),
            pltpu.VMEM((GX, 48, 128), BF16),
            pltpu.VMEM((NQ, GX, 48, 128), BF16),
            pltpu.VMEM((NZ, 2, 4, 128, 128), BF16),
            pltpu.VMEM((PAIRS, 256, DEGREES), BF16),
            pltpu.VMEM((256, 128), BF16),
            pltpu.VMEM((NQ, GX, 2, 2, 3, 16, 128), BF16),
            pltpu.VMEM((2, GX, 3, 16, 128), BF16),
            pltpu.VMEM((2, GX, 3, 16, 128), BF16),
            pltpu.VMEM((2, 2, PEERS, 3, 16, 128), BF16),
            pltpu.VMEM((2, 768, 512), BF16),
            pltpu.SemaphoreType.DMA,
            pltpu.SemaphoreType.DMA,
            pltpu.SemaphoreType.DMA((NQ, PAIRS, 2)),
            pltpu.SemaphoreType.DMA((2, 4)),
            pltpu.SemaphoreType.DMA((2, 4)),
            pltpu.SemaphoreType.DMA,
            pltpu.SemaphoreType.DMA((NQ // 2,)),
            pltpu.SemaphoreType.DMA,
            pltpu.SemaphoreType.DMA((NQ // 2,)),
            pltpu.SemaphoreType.DMA((2, 2, 4, 4)),
            pltpu.SemaphoreType.DMA((2, 2, 4, 4)),
            pltpu.SemaphoreType.DMA((2, 2)),
            pltpu.SemaphoreType.DMA((2, 2)),
            pltpu.SemaphoreType.DMA((2, 2)),
            pltpu.SemaphoreType.DMA((2, 2)),
            pltpu.SemaphoreType.DMA((2,)),
        ],
        compiler_params=pltpu.CompilerParams(
            collective_id=0, has_side_effects=True, vmem_limit_bytes=32 * 2**20
        ),
        cost_estimate=pl.CostEstimate(flops=2 * 10**9, bytes_accessed=10**7, transcendentals=0),
    )(*(pltpu.with_memory_space_constraint(a, pltpu.HBM) for a in (counts, spectra, legendre, perm)))


TILE = 256
STEPS = HALF // TILE
CHUNK = 16


def synthesis_kernel(field, geometry, left, table, out, factors, waves, stage, sems):
    squared = field[0]
    cos_theta = geometry[0]
    sin_theta = geometry[1]
    factors[0] = cos_theta
    factors[1] = sin_theta
    factors[2] = squared * cos_theta * sin_theta
    factors[3] = 0.5 * squared * sin_theta * sin_theta
    factors[4] = 2.0 * squared * cos_theta * cos_theta
    factors[5] = 0.5 * squared * (4.0 * cos_theta * cos_theta + sin_theta * sin_theta)

    def ship(i, h):
        return pltpu.make_async_copy(
            stage.at[i, h],
            out.at[0, :, :, pl.ds(h * HALF + i * TILE, TILE)],
            sems.at[i, h],
        )

    def wide(value):
        return jnp.concatenate([value] * (TILE // 128), axis=1)

    def transform(i):
        columns = pl.ds(i * TILE, TILE)
        for o in range(2):
            waves[i % 2, o] = jnp.dot(left[o], table[o, :, columns], preferred_element_type=F32)

    def finish(i):
        for r in range(0, NLAT_W, CHUNK):
            here = pl.ds(r, CHUNK)
            cos_w, sin_w, mix, own, twice, total = (wide(factors[n, here, :]) for n in range(6))
            even = [waves[i % 2, 0, pl.ds(128 * n + r, CHUNK), :] for n in range(6)]
            odd = [waves[i % 2, 1, pl.ds(128 * n + r, CHUNK), :] for n in range(6)]
            for h in range(2):
                flow = [a + b if h == 0 else a - b for a, b in zip(even, odd)]
                radial, polar, azimuth = flow[:3]
                stage[i, h, 0, here, :] = (
                    sin_w * azimuth + mix * polar - radial * (own + flow[3])
                ).astype(BF16)
                stage[i, h, 1, here, :] = (
                    cos_w * azimuth - twice * polar + radial * (mix - flow[4])
                ).astype(BF16)
                stage[i, h, 2, here, :] = (
                    -(cos_w * polar + total * azimuth + radial * (sin_w + flow[5]))
                ).astype(BF16)
        for h in range(2):
            ship(i, h).start()

    transform(0)
    for i in range(STEPS):
        if i + 1 < STEPS:
            transform(i + 1)
        finish(i)
    for i in range(STEPS):
        for h in range(2):
            ship(i, h).wait()


def synthesis(field, geometry, left, table):
    return pl.pallas_call(
        synthesis_kernel,
        out_shape=jax.ShapeDtypeStruct((1, 3, NLAT_W, LONGITUDE_COUNT), BF16),
        in_specs=[
            pl.BlockSpec(memory_space=pltpu.SMEM),
            pl.BlockSpec(memory_space=pltpu.VMEM),
            pl.BlockSpec(memory_space=pltpu.VMEM),
            pl.BlockSpec(memory_space=pltpu.VMEM),
        ],
        out_specs=pl.BlockSpec(memory_space=pl.ANY),
        scratch_shapes=[
            pltpu.VMEM((6, NLAT_W, 128), F32),
            pltpu.VMEM((2, 2, 768, TILE), F32),
            pltpu.VMEM((STEPS, 2, 3, NLAT_W, TILE), BF16),
            pltpu.SemaphoreType.DMA((STEPS, 2)),
        ],
        compiler_params=pltpu.CompilerParams(vmem_limit_bytes=32 * 2**20),
        cost_estimate=pl.CostEstimate(flops=3 * 10**9, bytes_accessed=7 * 10**6, transcendentals=0),
    )(field, geometry, left, table)


def shards(spectra, legendre, degree_counts):
    perm = jnp.asarray(order_permutation(), BF16)
    table = jnp.asarray(fourier_table(), BF16)
    theta = np.pi * (np.arange(NLAT_W) + (NLAT - NLAT_W) // 2 + 0.5) / NLAT
    geometry = np.repeat(np.stack([np.cos(theta), np.sin(theta)])[:, :, None], 128, axis=2)
    geometry = jnp.asarray(geometry, F32)
    shell = lax.axis_index(("grp", "sub")).astype(F32)
    radius = RADIUS_IN + (shell + 0.5) / SHELLS
    field = ((RADIUS_IN / radius) ** 6).reshape(1)
    left = exchange(degree_counts, spectra, legendre, perm)
    return synthesis(field, geometry, left, table)


def solution(mesh):
    in_specs = (P(("grp", "sub"), None, None, None), P("sub", None, None), P())
    out_specs = P(("grp", "sub"), None, None, None)
    return jax.shard_map(shards, mesh=mesh, in_specs=in_specs, out_specs=out_specs, check_vma=False)
```
